128 devices in a mesh: wide: 32 (over z, y, core), narrow: 4 (over x).
Axes of the slice: x: 4, y: 4, z: 4, core: 2. Of those that a mesh axis runs over, the one named last changes fastest.
Arguments:
- embeddings: float32 [16384, 1024], P(('wide', 'narrow')), may hold values from -6 to 6
- cluster: int32 [16384], P(('wide', 'narrow')), may hold values from 0 to 63, as said below
- order: int32 [16384], P(('wide', 'narrow')), may hold values from 0 to 511
Outputs:
- best_similarity: float32 [16384], P(('wide', 'narrow'))
The draws below stay inside these ranges and needn't reach their ends.
Inputs may be any that keep to these rules, and one draw needn't show every extreme that they name: Documents of one cluster have distinct order values. For every k, at most 8 documents of one device lie in clusters k * 2 to k * 2 + 1, and on every device exactly 8 for some k.
All inputs are finite; a program needn't handle non-finite values.
Results may differ from the reference program's by a relative error of at most 0.0013.
Values may be sent and summed in bfloat16 or wider, within the bound.
No kernel may reach another device: no remote copies, remote signals or barrier semaphores. Data moves between devices by JAX's collectives and lax.ppermute only.
A program may use at most 64 MiB of HBM per device.

```python
import jax
import jax.numpy as jnp
from jax import lax

E = 1024
DOC_DEV = 128
CL_DEV = 2
DOCS = 16384
CLUSTERS = 64
SEND_CAP = 8
CAP = 512


def layout_pair(key):
    owner_count = CLUSTERS // CL_DEV
    device_count = DOCS // DOC_DEV
    share = SEND_CAP // 2
    base_counts = jnp.concatenate([jnp.full((owner_count // 4,), SEND_CAP, jnp.int32), jnp.full((owner_count // 2,), share, jnp.int32), jnp.full((owner_count // 4,), 0, jnp.int32)])
    count_keys = jax.random.split(jax.random.fold_in(key, 11), device_count)
    counts = jax.vmap(lambda sub_key: jax.random.permutation(sub_key, base_counts))(count_keys)
    offsets = (jnp.cumsum(counts, axis=1) - counts).astype(jnp.int32)
    doc_pos = jnp.arange(DOC_DEV, dtype=jnp.int32)
    owner_of = (jnp.sum((doc_pos[None, :, None] >= offsets[:, None, :]).astype(jnp.int32), axis=2) - 1).astype(jnp.int32)
    within = doc_pos[None, :] - jnp.take_along_axis(offsets, owner_of, axis=1)
    local_cluster = within // share
    sub_pos = within % share
    device_ids = jnp.arange(device_count, dtype=jnp.int32)[:, None]
    position = device_ids * share + sub_pos
    cluster_of = (owner_of * CL_DEV + local_cluster).astype(jnp.int32)
    perm_keys = jax.random.split(jax.random.fold_in(key, 12), CLUSTERS)
    perms = jax.vmap(lambda sub_key: jax.random.permutation(sub_key, CAP))(perm_keys).astype(jnp.int32)
    rank_of = perms[cluster_of, position].astype(jnp.int32)
    shuffle_keys = jax.random.split(jax.random.fold_in(key, 13), device_count)
    shuffles = jax.vmap(lambda sub_key: jax.random.permutation(sub_key, DOC_DEV))(shuffle_keys).astype(jnp.int32)
    cluster_of = jnp.take_along_axis(cluster_of, shuffles, axis=1)
    rank_of = jnp.take_along_axis(rank_of, shuffles, axis=1)
    return (cluster_of.reshape(-1).astype(jnp.int32), rank_of.reshape(-1).astype(jnp.int32))


def draw_cluster(key, part):
    return layout_pair(key)[0]


def draw_order(key, part):
    return layout_pair(key)[1]


def level_of(key, extent, cuts, smallest, largest):
    level = 1.0
    for axis_at, parts in cuts:
        steps = jax.random.uniform(jax.random.fold_in(jax.random.fold_in(key, 6), axis_at), (parts,), jnp.float32, smallest / len(cuts), largest / len(cuts))
        level = level * jnp.repeat(jnp.exp(steps), extent[axis_at] // parts).reshape((-1,) + (1,) * (len(extent) - 1 - axis_at))
    return level


def normal_values(stream_key, extent, spread, most, cuts=(), kind=jnp.bfloat16):
    values = jax.random.normal(stream_key, extent, jnp.float32) * spread
    if len(cuts) > 0:
        values = level_of(stream_key, extent, cuts, -0.22, 0.18) * values
    return jnp.clip(values, min=-most, max=most).astype(kind)


def setup_inputs(seed: int = 0) -> dict:
    arg_keys = jax.random.split(jax.random.key(seed), 4)
    embeddings = normal_values(arg_keys[0], (DOCS, E), 1.0, 6.0, ((0, 128),), jnp.float32)
    cluster = draw_cluster(jax.random.fold_in(arg_keys[3], 71), 0)
    order = draw_order(jax.random.fold_in(arg_keys[3], 71), 0)
    return {"embeddings": embeddings, "cluster": cluster, "order": order}


epsilon = 1e-06

def reference(embeddings, cluster, order):
    squares = lax.optimization_barrier(jnp.sum(embeddings * embeddings, axis=1, keepdims=True))
    unit_rows = (embeddings * lax.rsqrt(squares + epsilon)).astype(jnp.bfloat16)
    slot_index = (cluster * CAP + order).astype(jnp.int32)
    slot_table = jnp.zeros((CLUSTERS * CAP, E), jnp.bfloat16).at[slot_index].set(unit_rows)
    slot_live = jnp.zeros((CLUSTERS * CAP,), jnp.float32).at[slot_index].set(1.0)
    slot_table = slot_table.reshape(CLUSTERS, CAP, E)
    slot_live = slot_live.reshape(CLUSTERS, CAP)

    def cluster_best(operands):
        members, member_live = operands
        wide_rows = members.astype(jnp.float32)
        similar = jnp.dot(wide_rows, wide_rows.T)
        positions = jnp.arange(CAP, dtype=jnp.int32)
        allowed = (positions[None, :] < positions[:, None]) & (member_live[None, :] > 0)
        return lax.optimization_barrier(jnp.max(jnp.where(allowed, similar, jnp.float32(-1.0)), axis=1))
    best_value = lax.map(cluster_best, (slot_table, slot_live)).reshape(-1)
    return best_value[slot_index]
```

```python
import jax
import jax.numpy as jnp
from jax import lax
from jax.experimental import pallas as pl
from jax.experimental.pallas import tpu as pltpu
from jax.sharding import Mesh, PartitionSpec as P

CLUSTERS = 64
SLOTS = 8
CAP = 512
LANES = 128
CORES = 2
epsilon = 1e-06

VMEM = 32 * 1024 * 1024
NT = (((1,), (1,)), ((), ()))
TN = (((0,), (0,)), ((), ()))


def iota(shape, axis):
    return lax.broadcasted_iota(jnp.int32, shape, axis)


def as_bf16(mask):
    return jnp.where(mask, 1.0, 0.0).astype(jnp.bfloat16)


def pack_kernel(rows_ref, cluster_ref, order_ref, out_ref, position_ref):
    docs, width = rows_ref.shape
    slots = out_ref.shape[0]
    cluster = cluster_ref[...]
    member = iota((CLUSTERS, docs), 0) == cluster
    before = as_bf16(iota((docs, docs), 0) < iota((docs, docs), 1))
    count = jnp.dot(as_bf16(member), before, preferred_element_type=jnp.float32)
    position = jnp.sum(jnp.where(member, count, 0.0), axis=0, keepdims=True).astype(jnp.int32)
    position_ref[...] = position
    target = cluster * SLOTS + position
    place = as_bf16(iota((slots, docs), 0) == target)
    rank = order_ref[...] - CAP
    high = (rank >> 4).astype(jnp.float32)
    low = (rank & 15).astype(jnp.float32)
    line = iota((LANES, docs), 0)
    ranks = jnp.where(line == 0, high, jnp.where(line == 1, low, 0.0)).astype(jnp.bfloat16)
    out_ref[:, width:] = lax.dot_general(
        place, ranks, NT, preferred_element_type=jnp.float32
    ).astype(jnp.bfloat16)
    rows = rows_ref[...]
    squares = jnp.sum(rows * rows, axis=1, keepdims=True)
    unit = (rows * lax.rsqrt(squares + epsilon)).astype(jnp.bfloat16)
    out_ref[:, :width] = jnp.dot(place, unit, preferred_element_type=jnp.float32).astype(
        jnp.bfloat16
    )


def best_of(query_ref, key_ref, width, first):
    keys = key_ref.shape[0]
    weight_lane = iota((8, LANES), 1)
    weight = jnp.where(weight_lane == 0, 16.0, jnp.where(weight_lane == 1, 1.0, 0.0)).astype(
        jnp.bfloat16
    )
    key_rank = lax.dot_general(
        weight, key_ref[:, width:], NT, preferred_element_type=jnp.float32
    )[0:1]
    spread_line = iota((LANES, LANES), 0)
    spread = jnp.where(spread_line == 0, 16.0, jnp.where(spread_line == 1, 1.0, 0.0)).astype(
        jnp.bfloat16
    )
    query_rank = jnp.dot(query_ref[:, width:], spread, preferred_element_type=jnp.float32)
    similar = lax.dot_general(
        query_ref[:, :width], key_ref[:, :width], NT, preferred_element_type=jnp.float32
    )
    best = first
    for at in range(0, keys, LANES):
        allowed = key_rank[:, at : at + LANES] < query_rank
        best = jnp.maximum(best, jnp.where(allowed, similar[:, at : at + LANES], -1.0))
    return best


def own_kernel(own_ref, best_ref):
    width = own_ref.shape[1] - LANES
    best_ref[...] = best_of(own_ref, own_ref, width, jnp.float32(-1.0))


def other_kernel(own_ref, other_ref, first_ref, out_ref):
    width = own_ref.shape[1] - LANES
    best = best_of(own_ref, other_ref, width, first_ref[...])
    best = jnp.max(best, axis=1, keepdims=True)
    slots = own_ref.shape[0]
    mine = iota((slots, LANES), 1) == iota((slots, LANES), 0) % SLOTS
    spread = jnp.where(mine, best, 0.0).reshape(slots // SLOTS, SLOTS, LANES)
    out_ref[...] = jnp.sum(spread, axis=1)


def unpack_kernel(best_ref, cluster_ref, position_ref, out_ref):
    docs = cluster_ref.shape[1]
    member = jnp.where(iota((CLUSTERS, docs), 0) == cluster_ref[...], 1.0, 0.0)
    by_slot = lax.dot_general(
        best_ref[...],
        member,
        TN,
        precision=lax.Precision.HIGHEST,
        preferred_element_type=jnp.float32,
    )
    wanted = iota((LANES, docs), 0) == position_ref[...]
    out_ref[...] = jnp.sum(jnp.where(wanted, by_slot, 0.0), axis=0, keepdims=True)


def call(kernel, out_shape, flops, moved):
    return pl.pallas_call(
        kernel,
        out_shape=out_shape,
        compiler_params=pltpu.CompilerParams(vmem_limit_bytes=VMEM),
        cost_estimate=pl.CostEstimate(flops=flops, bytes_accessed=moved, transcendentals=0),
    )


def per_device(embeddings, cluster, order):
    docs, width = embeddings.shape
    slots = CLUSTERS * SLOTS
    wide = width + LANES
    f32 = jnp.float32
    cluster, order = cluster.reshape(1, docs), order.reshape(1, docs)
    packed, position = call(
        pack_kernel,
        (
            jax.ShapeDtypeStruct((slots, wide), jnp.bfloat16),
            jax.ShapeDtypeStruct((1, docs), jnp.int32),
        ),
        2 * slots * docs * wide,
        docs * width * 4 + slots * wide * 2,
    )(embeddings, cluster, order)
    own = lax.all_to_all(packed, ("zy", "x"), split_axis=0, concat_axis=0, tiled=True)
    other = lax.ppermute(own, "core", [(0, 1), (1, 0)])
    flops = 2 * slots * slots * width
    first = call(
        own_kernel, jax.ShapeDtypeStruct((slots, LANES), f32), flops, slots * wide * 2
    )(own)
    best = call(
        other_kernel,
        jax.ShapeDtypeStruct((CLUSTERS, LANES), f32),
        flops,
        2 * slots * wide * 2,
    )(own, other, first)
    back = lax.all_to_all(best, ("zy", "x"), split_axis=0, concat_axis=0, tiled=True)
    result = call(
        unpack_kernel, jax.ShapeDtypeStruct((1, docs), f32), 0, CLUSTERS * LANES * 4
    )(back, cluster, position)
    return result.reshape(docs)


def solution(mesh):
    devices = mesh.devices.reshape(-1, CORES, mesh.shape["narrow"])
    chips = Mesh(devices, ("zy", "core", "x"))
    axes = ("zy", "core", "x")
    return jax.shard_map(
        per_device,
        mesh=chips,
        in_specs=(P(axes, None), P(axes), P(axes)),
        out_specs=P(axes),
        check_vma=False,
    )
```

```python
import jax
import jax.numpy as jnp
from jax import lax
from jax.experimental import pallas as pl
from jax.experimental.pallas import tpu as pltpu
from jax.sharding import Mesh, PartitionSpec as P

CLUSTERS = 64
SLOTS = 8
CAP = 512
LANES = 128
CORES = 2
epsilon = 1e-06

VMEM = 32 * 1024 * 1024
NT = (((1,), (1,)), ((), ()))


def iota(shape, axis):
    return lax.broadcasted_iota(jnp.int32, shape, axis)


def as_bf16(mask):
    return jnp.where(mask, 1.0, 0.0).astype(jnp.bfloat16)


def pack_kernel(rows_hbm, cluster_hbm, order_hbm, out_ref, where_ref, rows_ref, ids_ref, sems):
    docs, width = rows_ref.shape
    slots = out_ref.shape[0]
    cluster_copy = pltpu.make_async_copy(cluster_hbm, ids_ref.at[0], sems.at[0])
    order_copy = pltpu.make_async_copy(order_hbm, ids_ref.at[1], sems.at[1])
    rows_copy = pltpu.make_async_copy(rows_hbm, rows_ref, sems.at[2])
    cluster_copy.start()
    order_copy.start()
    rows_copy.start()
    before = as_bf16(iota((docs, docs), 0) < iota((docs, docs), 1))
    line = iota((LANES, docs), 0)
    slot = iota((slots, docs), 0)
    cluster_copy.wait()
    order_copy.wait()
    cluster = ids_ref[0]
    member = iota((CLUSTERS, docs), 0) == cluster
    count = jnp.dot(as_bf16(member), before, preferred_element_type=jnp.float32)
    position = jnp.sum(jnp.where(member, count, 0.0), axis=0, keepdims=True).astype(jnp.int32)
    where_ref[0:1] = cluster
    where_ref[1:2] = position
    place = as_bf16(slot == cluster * SLOTS + position)
    rank = ids_ref[1] - CAP
    high = (rank >> 4).astype(jnp.float32)
    low = (rank & 15).astype(jnp.float32)
    ranks = jnp.where(line == 0, high, jnp.where(line == 1, low, 0.0)).astype(jnp.bfloat16)
    out_ref[:, width:] = lax.dot_general(
        place, ranks, NT, preferred_element_type=jnp.float32
    ).astype(jnp.bfloat16)
    rows_copy.wait()
    rows = rows_ref[...]
    squares = jnp.sum(rows * rows, axis=1, keepdims=True)
    unit = (rows * lax.rsqrt(squares + epsilon)).astype(jnp.bfloat16)
    out_ref[:, :width] = jnp.dot(place, unit, preferred_element_type=jnp.float32).astype(
        jnp.bfloat16
    )


def rank_weights(shape, axis):
    at = iota(shape, axis)
    return jnp.where(at == 0, 16.0, jnp.where(at == 1, 1.0, 0.0)).astype(jnp.bfloat16)


def best_of(keys_ref, queries_ref, rank_ref, width, first):
    keys = keys_ref.shape[0]
    key_rank = jnp.dot(
        keys_ref[:, width:],
        rank_weights((LANES, LANES), 0),
        preferred_element_type=jnp.float32,
    )
    step = 2 * LANES
    best = []
    for at in range(0, queries_ref.shape[1], step):
        similar = jnp.dot(
            keys_ref[:, :width],
            queries_ref[:, at : at + step],
            preferred_element_type=jnp.float32,
        )
        for lane in range(0, step, LANES):
            allowed = key_rank < rank_ref[0:1, at + lane : at + lane + LANES]
            value = jnp.where(allowed, similar[:, lane : lane + LANES], -1.0)
            value = jnp.max(value.reshape(keys // 8, 8, LANES), axis=0)
            best.append(jnp.maximum(value, first[:, at + lane : at + lane + LANES]))
    return best


def own_kernel(own_ref, queries_ref, rank_ref, best_ref):
    slots, width = own_ref.shape[0], own_ref.shape[1] - LANES
    queries_ref[...] = own_ref[:, :width].T
    rank_ref[...] = lax.dot_general(
        rank_weights((8, LANES), 1), own_ref[:, width:], NT, preferred_element_type=jnp.float32
    )
    first = jnp.full((8, slots), -1.0, jnp.float32)
    for at, best in enumerate(best_of(own_ref, queries_ref, rank_ref, width, first)):
        best_ref[:, at * LANES : (at + 1) * LANES] = best


def other_kernel(other_ref, queries_ref, rank_ref, first_ref, out_ref):
    width = queries_ref.shape[0]
    lines = LANES // SLOTS
    for at, best in enumerate(best_of(other_ref, queries_ref, rank_ref, width, first_ref[...])):
        best = jnp.max(best, axis=0, keepdims=True)
        out_ref[at * lines : (at + 1) * lines] = jnp.broadcast_to(best, (lines, LANES))


def unpack_kernel(chip_ref, best_ref, where_ref, out_ref, turned_ref):
    docs = where_ref.shape[1]
    best = jnp.concatenate([best_ref[...], jnp.zeros((LANES - CLUSTERS, LANES), jnp.float32)])
    turned_ref[...] = best.T
    start = pl.multiple_of(chip_ref[0] % (LANES // SLOTS) * SLOTS, SLOTS)
    mine = turned_ref[pl.ds(start, SLOTS)]
    cluster = jnp.broadcast_to(where_ref[0:1], (SLOTS, docs))
    by_cluster = jnp.take_along_axis(mine, cluster, axis=1)
    wanted = iota((SLOTS, docs), 0) == where_ref[1:2]
    out_ref[...] = jnp.sum(jnp.where(wanted, by_cluster, 0.0), axis=0, keepdims=True)


def call(kernel, out_shape, flops, moved, **more):
    return pl.pallas_call(
        kernel,
        out_shape=out_shape,
        compiler_params=pltpu.CompilerParams(vmem_limit_bytes=VMEM),
        cost_estimate=pl.CostEstimate(flops=flops, bytes_accessed=moved, transcendentals=0),
        **more,
    )


def per_device(embeddings, cluster, order):
    docs, width = embeddings.shape
    slots = CLUSTERS * SLOTS
    wide = width + LANES
    shape = jax.ShapeDtypeStruct
    f32, bf16, i32 = jnp.float32, jnp.bfloat16, jnp.int32
    packed, where = call(
        pack_kernel,
        (shape((slots, wide), bf16), shape((8, docs), i32)),
        2 * slots * docs * wide,
        docs * width * 4 + slots * wide * 2,
        in_specs=[pl.BlockSpec(memory_space=pltpu.HBM)] * 3,
        scratch_shapes=[
            pltpu.VMEM((docs, width), f32),
            pltpu.VMEM((2, 1, docs), i32),
            pltpu.SemaphoreType.DMA((3,)),
        ],
    )(embeddings, cluster.reshape(1, docs), order.reshape(1, docs))
    own = lax.all_to_all(packed, ("zy", "x"), split_axis=0, concat_axis=0, tiled=True)
    other = lax.ppermute(own, "core", [(0, 1), (1, 0)])
    flops = 2 * slots * slots * width
    queries, rank, first = call(
        own_kernel,
        (shape((width, slots), bf16), shape((8, slots), f32), shape((8, slots), f32)),
        flops,
        2 * slots * wide * 2,
    )(own)
    best = call(other_kernel, shape((CLUSTERS, LANES), f32), flops, 2 * slots * wide * 2)(
        other, queries, rank, first
    )
    back = lax.all_to_all(best, ("zy", "x"), split_axis=0, concat_axis=0, tiled=True)
    chip = lax.axis_index(("zy", "x")).astype(i32).reshape(1)
    vmem = pl.BlockSpec(memory_space=pltpu.VMEM)
    result = call(
        unpack_kernel,
        shape((1, docs), f32),
        0,
        CLUSTERS * LANES * 4,
        in_specs=[pl.BlockSpec(memory_space=pltpu.SMEM), vmem, vmem],
        scratch_shapes=[pltpu.VMEM((LANES, LANES), f32)],
    )(chip, back, where)
    return result.reshape(docs)


def solution(mesh):
    devices = mesh.devices.reshape(-1, CORES, mesh.shape["narrow"])
    chips = Mesh(devices, ("zy", "core", "x"))
    axes = ("zy", "core", "x")
    return jax.shard_map(
        per_device,
        mesh=chips,
        in_specs=(P(axes, None), P(axes), P(axes)),
        out_specs=P(axes),
        check_vma=False,
    )
```

```python
import jax
import jax.numpy as jnp
from jax import lax
from jax.experimental import pallas as pl
from jax.experimental.pallas import tpu as pltpu
from jax.sharding import Mesh, PartitionSpec as P

CLUSTERS = 64
SLOTS = 8
CAP = 512
LANES = 128
CORES = 2
epsilon = 1e-06

VMEM = 32 * 1024 * 1024
NT = (((1,), (1,)), ((), ()))


def iota(shape, axis):
    return lax.broadcasted_iota(jnp.int32, shape, axis)


def as_bf16(mask):
    return jnp.where(mask, 1.0, 0.0).astype(jnp.bfloat16)


def pack_kernel(rows_hbm, cluster_hbm, order_hbm, out_ref, where_ref, rows_ref, ids_ref, sems):
    docs, width = rows_ref.shape
    slots = out_ref.shape[0]
    cluster_copy = pltpu.make_async_copy(cluster_hbm, ids_ref.at[0], sems.at[0])
    order_copy = pltpu.make_async_copy(order_hbm, ids_ref.at[1], sems.at[1])
    rows_copy = pltpu.make_async_copy(rows_hbm, rows_ref, sems.at[2])
    cluster_copy.start()
    order_copy.start()
    rows_copy.start()
    before = as_bf16(iota((docs, docs), 0) < iota((docs, docs), 1))
    line = iota((LANES, docs), 0)
    slot = iota((slots, docs), 0)
    cluster_copy.wait()
    order_copy.wait()
    cluster = ids_ref[0]
    member = iota((CLUSTERS, docs), 0) == cluster
    count = jnp.dot(as_bf16(member), before, preferred_element_type=jnp.float32)
    position = jnp.sum(jnp.where(member, count, 0.0), axis=0, keepdims=True).astype(jnp.int32)
    chip = lax.axis_index("zy") * lax.axis_size("x") + lax.axis_index("x")
    where_ref[0:1] = cluster
    where_ref[1:2] = chip % (LANES // SLOTS) * SLOTS + position
    place = as_bf16(slot == cluster * SLOTS + position)
    rank = ids_ref[1] - CAP
    high = (rank >> 4).astype(jnp.float32)
    low = (rank & 15).astype(jnp.float32)
    ranks = jnp.where(line == 0, high, jnp.where(line == 1, low, 0.0)).astype(jnp.bfloat16)
    out_ref[:, width:] = lax.dot_general(
        place, ranks, NT, preferred_element_type=jnp.float32
    ).astype(jnp.bfloat16)
    rows_copy.wait()
    rows = rows_ref[...]
    squares = jnp.sum(rows * rows, axis=1, keepdims=True)
    unit = (rows * lax.rsqrt(squares + epsilon)).astype(jnp.bfloat16)
    out_ref[:, :width] = jnp.dot(place, unit, preferred_element_type=jnp.float32).astype(
        jnp.bfloat16
    )


def rank_weights(shape, axis):
    at = iota(shape, axis)
    return jnp.where(at == 0, 16.0, jnp.where(at == 1, 1.0, 0.0)).astype(jnp.bfloat16)


def best_of(keys_ref, queries_ref, rank_ref, width, first):
    keys = keys_ref.shape[0]
    key_rank = jnp.dot(
        keys_ref[:, width:],
        rank_weights((LANES, LANES), 0),
        preferred_element_type=jnp.float32,
    )
    step = 2 * LANES
    best = []
    for at in range(0, queries_ref.shape[1], step):
        similar = jnp.dot(
            keys_ref[:, :width],
            queries_ref[:, at : at + step],
            preferred_element_type=jnp.float32,
        )
        for lane in range(0, step, LANES):
            allowed = key_rank < rank_ref[0:1, at + lane : at + lane + LANES]
            value = jnp.where(allowed, similar[:, lane : lane + LANES], -1.0)
            value = jnp.max(value.reshape(keys // 8, 8, LANES), axis=0)
            best.append(jnp.maximum(value, first[:, at + lane : at + lane + LANES]))
    return best


def own_kernel(own_ref, queries_ref, rank_ref, best_ref):
    slots, width = own_ref.shape[0], own_ref.shape[1] - LANES
    queries_ref[...] = own_ref[:, :width].T
    rank_ref[...] = lax.dot_general(
        rank_weights((8, LANES), 1), own_ref[:, width:], NT, preferred_element_type=jnp.float32
    )
    first = jnp.full((8, slots), -1.0, jnp.float32)
    for at, best in enumerate(best_of(own_ref, queries_ref, rank_ref, width, first)):
        best_ref[:, at * LANES : (at + 1) * LANES] = best


def other_kernel(other_ref, queries_ref, rank_ref, first_ref, out_ref):
    width = queries_ref.shape[0]
    lines = LANES // SLOTS
    for at, best in enumerate(best_of(other_ref, queries_ref, rank_ref, width, first_ref[...])):
        best = jnp.max(best, axis=0, keepdims=True)
        out_ref[at * lines : (at + 1) * lines] = jnp.broadcast_to(best, (lines, LANES))


def unpack_kernel(best_ref, where_ref, out_ref):
    docs = where_ref.shape[1]
    best = jnp.concatenate([best_ref[...], jnp.zeros((LANES - CLUSTERS, LANES), jnp.float32)])
    cluster = jnp.broadcast_to(where_ref[0:1], (LANES, docs))
    by_cluster = jnp.take_along_axis(best.T, cluster, axis=1)
    wanted = iota((LANES, docs), 0) == where_ref[1:2]
    out_ref[...] = jnp.sum(jnp.where(wanted, by_cluster, 0.0), axis=0, keepdims=True)


def call(kernel, out_shape, flops, moved, **more):
    return pl.pallas_call(
        kernel,
        out_shape=out_shape,
        compiler_params=pltpu.CompilerParams(vmem_limit_bytes=VMEM),
        cost_estimate=pl.CostEstimate(flops=flops, bytes_accessed=moved, transcendentals=0),
        **more,
    )


def in_hbm(x):
    return pltpu.with_memory_space_constraint(x, pltpu.HBM)


def per_device(embeddings, cluster, order):
    docs, width = embeddings.shape
    slots = CLUSTERS * SLOTS
    wide = width + LANES
    shape = jax.ShapeDtypeStruct
    f32, bf16, i32 = jnp.float32, jnp.bfloat16, jnp.int32
    packed, where = call(
        pack_kernel,
        (shape((slots, wide), bf16), shape((8, docs), i32)),
        2 * slots * docs * wide,
        docs * width * 4 + slots * wide * 2,
        in_specs=[pl.BlockSpec(memory_space=pltpu.HBM)] * 3,
        scratch_shapes=[
            pltpu.VMEM((docs, width), f32),
            pltpu.VMEM((2, 1, docs), i32),
            pltpu.SemaphoreType.DMA((3,)),
        ],
    )(*(in_hbm(x) for x in (embeddings, cluster.reshape(1, docs), order.reshape(1, docs))))
    own = lax.all_to_all(packed, ("zy", "x"), split_axis=0, concat_axis=0, tiled=True)
    other = lax.ppermute(own, "core", [(0, 1), (1, 0)])
    flops = 2 * slots * slots * width
    queries, rank, first = call(
        own_kernel,
        (shape((width, slots), bf16), shape((8, slots), f32), shape((8, slots), f32)),
        flops,
        2 * slots * wide * 2,
    )(own)
    best = call(other_kernel, shape((CLUSTERS, LANES), f32), flops, 2 * slots * wide * 2)(
        other, queries, rank, first
    )
    back = lax.all_to_all(best, ("zy", "x"), split_axis=0, concat_axis=0, tiled=True)
    result = call(unpack_kernel, shape((1, docs), f32), 0, CLUSTERS * LANES * 4)(back, where)
    return result.reshape(docs)


def solution(mesh):
    devices = mesh.devices.reshape(-1, CORES, mesh.shape["narrow"])
    chips = Mesh(devices, ("zy", "core", "x"))
    axes = ("zy", "core", "x")
    return jax.shard_map(
        per_device,
        mesh=chips,
        in_specs=(P(axes, None), P(axes), P(axes)),
        out_specs=P(axes),
        check_vma=False,
    )
```

```python
import jax
import jax.numpy as jnp
from jax import lax
from jax.experimental import pallas as pl
from jax.experimental.pallas import tpu as pltpu
from jax.sharding import Mesh, PartitionSpec as P

CLUSTERS = 64
SLOTS = 8
CAP = 512
LANES = 128
CORES = 2
CHUNKS = 4
GROUPS = CLUSTERS // CHUNKS
PART = GROUPS * SLOTS
TILES = 33
epsilon = 1e-06

VMEM = 32 * 1024 * 1024
NT = (((1,), (1,)), ((), ()))


def iota(shape, axis):
    return lax.broadcasted_iota(jnp.int32, shape, axis)


def as_bf16(mask):
    return jnp.where(mask, 1.0, 0.0).astype(jnp.bfloat16)


def pack_kernel(rows_hbm, cluster_hbm, order_hbm, out_ref, where_ref, rows_ref, ids_ref, sems):
    docs, width = rows_ref.shape
    cluster_copy = pltpu.make_async_copy(cluster_hbm, ids_ref.at[0], sems.at[0])
    order_copy = pltpu.make_async_copy(order_hbm, ids_ref.at[1], sems.at[1])
    rows_copy = pltpu.make_async_copy(rows_hbm, rows_ref, sems.at[2])
    cluster_copy.start()
    order_copy.start()
    rows_copy.start()
    before = as_bf16(iota((docs, docs), 0) < iota((docs, docs), 1))
    cluster_copy.wait()
    order_copy.wait()
    cluster = ids_ref[0]
    member = iota((CLUSTERS, docs), 0) == cluster
    count = jnp.dot(as_bf16(member), before, preferred_element_type=jnp.float32)
    position = jnp.sum(jnp.where(member, count, 0.0), axis=0, keepdims=True).astype(jnp.int32)
    chip = lax.axis_index("zy") * lax.axis_size("x") + lax.axis_index("x")
    where_ref[0:1] = cluster
    where_ref[1:2] = chip // CHUNKS * SLOTS + (chip % CHUNKS * 2 + position) % SLOTS
    chunk = cluster % CHUNKS
    start = chunk * PART + cluster // CHUNKS * SLOTS
    line = iota((CHUNKS * PART, docs), 0)
    place = as_bf16(line == start + (chunk * 2 + position) % SLOTS)
    rank = ids_ref[1] - CAP
    high = (rank >> 4).astype(jnp.float32)
    low = (rank & 15).astype(jnp.float32)
    high_line = start + chunk * 2
    marks = jnp.where(line == high_line, high, jnp.where(line == high_line + 1, low, 0.0))
    marks = lax.dot_general(
        marks.astype(jnp.bfloat16),
        as_bf16(iota((LANES, docs), 0) == position),
        NT,
        preferred_element_type=jnp.float32,
    )
    rows_copy.wait()
    rows = rows_ref[...]
    squares = jnp.sum(rows * rows, axis=1, keepdims=True)
    unit = (rows * lax.rsqrt(squares + epsilon)).astype(jnp.bfloat16)
    slot = iota((GROUPS, SLOTS, LANES), 1)
    carried = None
    for at in range(CHUNKS):
        part = slice(at * PART, (at + 1) * PART)
        packed = jnp.dot(place[part], unit, preferred_element_type=jnp.float32)
        mine = slot >= at * 2
        for lane in range(0, width, LANES):
            tile = packed[:, lane : lane + LANES].reshape(GROUPS, SLOTS, LANES)
            value = tile if carried is None else jnp.where(mine, tile, carried)
            out_ref[:, at * 8 + lane // LANES] = value.astype(jnp.bfloat16)
            carried = tile
        mark = marks[part].reshape(GROUPS, SLOTS, LANES)
        carried = jnp.where(mine, mark, carried)
    out_ref[:, TILES - 1] = carried.astype(jnp.bfloat16)


def unfold(ref):
    slot = iota((GROUPS, SLOTS, LANES), 1)
    lane = iota((GROUPS, SLOTS, LANES), 2)
    rows, ranks = [], []
    for chunk in range(CHUNKS):
        turn = chunk * 2
        tiles = [ref[:, chunk * 8 + i] for i in range(9)]
        if chunk > 0:
            line = slot.astype(jnp.float32).astype(jnp.bfloat16)
            mine = line >= jnp.asarray(turn, jnp.bfloat16)
            data = [jnp.where(mine, x, y) for x, y in zip(tiles[:-1], tiles[1:])]
        else:
            data = tiles[:-1]
        rows.append(jnp.concatenate([x.reshape(PART, LANES) for x in data], axis=1))
        marks = tiles[-1].astype(jnp.float32)
        rank = marks[:, turn : turn + 1] * 16.0 + marks[:, turn + 1 : turn + 2]
        mine = lane == (slot - turn) % SLOTS
        rank = jnp.sum(jnp.where(mine, rank, 0.0), axis=2, keepdims=True)
        ranks.append(jnp.broadcast_to(rank, (GROUPS, SLOTS, LANES)).reshape(PART, LANES))
    return jnp.concatenate(rows, axis=0), jnp.concatenate(ranks, axis=0)


def best_of(keys, key_rank, queries_ref, rank_ref, first):
    step = 2 * LANES
    best = []
    for at in range(0, queries_ref.shape[1], step):
        similar = jnp.dot(
            keys, queries_ref[:, at : at + step], preferred_element_type=jnp.float32
        )
        for lane in range(0, step, LANES):
            allowed = key_rank < rank_ref[0:1, at + lane : at + lane + LANES]
            value = jnp.where(allowed, similar[:, lane : lane + LANES], -1.0)
            value = jnp.max(value.reshape(-1, 8, LANES), axis=0)
            best.append(jnp.maximum(value, first[:, at + lane : at + lane + LANES]))
    return best


def own_kernel(own_ref, queries_ref, rank_ref, best_ref):
    rows, ranks = unfold(own_ref)
    queries_ref[...] = rows.T
    rank_ref[...] = ranks.T[0:8]
    first = jnp.full(best_ref.shape, -1.0, jnp.float32)
    for at, best in enumerate(best_of(rows, ranks, queries_ref, rank_ref, first)):
        best_ref[:, at * LANES : (at + 1) * LANES] = best


def other_kernel(other_ref, queries_ref, rank_ref, first_ref, out_ref):
    rows, ranks = unfold(other_ref)
    best = best_of(rows, ranks, queries_ref, rank_ref, first_ref[...])
    lines = jnp.concatenate([jnp.max(x, axis=0, keepdims=True) for x in best])
    lines = jnp.concatenate([lines, lines])
    for at in range(0, CLUSTERS, 8):
        out_ref[at : at + 8] = lines


def unpack_kernel(best_ref, where_ref, out_ref):
    docs = where_ref.shape[1]
    best = jnp.concatenate([best_ref[...], jnp.zeros((LANES - CLUSTERS, LANES), jnp.float32)])
    cluster = jnp.broadcast_to(where_ref[0:1], (LANES, docs))
    by_cluster = jnp.take_along_axis(best.T, cluster, axis=1)
    wanted = iota((LANES, docs), 0) == where_ref[1:2]
    out_ref[...] = jnp.sum(jnp.where(wanted, by_cluster, 0.0), axis=0, keepdims=True)


def call(kernel, out_shape, flops, moved, **more):
    return pl.pallas_call(
        kernel,
        out_shape=out_shape,
        compiler_params=pltpu.CompilerParams(vmem_limit_bytes=VMEM),
        cost_estimate=pl.CostEstimate(flops=flops, bytes_accessed=moved, transcendentals=0),
        **more,
    )


def in_hbm(x):
    return pltpu.with_memory_space_constraint(x, pltpu.HBM)


def per_device(embeddings, cluster, order):
    docs, width = embeddings.shape
    slots = CLUSTERS * SLOTS
    shape = jax.ShapeDtypeStruct
    f32, bf16, i32 = jnp.float32, jnp.bfloat16, jnp.int32
    tiles = (GROUPS, TILES, 8, LANES)
    moved = CLUSTERS * (SLOTS * width + 2 * LANES) * 2
    packed, where = call(
        pack_kernel,
        (shape(tiles, bf16), shape((8, docs), i32)),
        2 * slots * docs * width,
        docs * width * 4 + moved,
        in_specs=[pl.BlockSpec(memory_space=pltpu.HBM)] * 3,
        scratch_shapes=[
            pltpu.VMEM((docs, width), f32),
            pltpu.VMEM((2, 1, docs), i32),
            pltpu.SemaphoreType.DMA((3,)),
        ],
    )(*(in_hbm(x) for x in (embeddings, cluster.reshape(1, docs), order.reshape(1, docs))))
    chunks = packed.reshape(CLUSTERS, TILES, 2, LANES)
    own = lax.all_to_all(chunks, ("zy", "x"), split_axis=0, concat_axis=0, tiled=True)
    other = lax.ppermute(own, "core", [(0, 1), (1, 0)])
    flops = 2 * slots * slots * width
    queries, rank, first = call(
        own_kernel,
        (shape((width, slots), bf16), shape((8, slots), f32), shape((8, slots), f32)),
        flops,
        2 * moved,
    )(own.reshape(tiles))
    best = call(other_kernel, shape((CLUSTERS, LANES), f32), flops, 2 * moved)(
        other.reshape(tiles), queries, rank, first
    )
    back = lax.all_to_all(best, ("zy", "x"), split_axis=0, concat_axis=0, tiled=True)
    result = call(unpack_kernel, shape((1, docs), f32), 0, CLUSTERS * LANES * 4)(back, where)
    return result.reshape(docs)


def solution(mesh):
    devices = mesh.devices.reshape(-1, CORES, mesh.shape["narrow"])
    chips = Mesh(devices, ("zy", "core", "x"))
    axes = ("zy", "core", "x")
    return jax.shard_map(
        per_device,
        mesh=chips,
        in_specs=(P(axes, None), P(axes), P(axes)),
        out_specs=P(axes),
        check_vma=False,
    )
```

```python
import jax
import jax.numpy as jnp
from jax import lax
from jax.experimental import pallas as pl
from jax.experimental.pallas import tpu as pltpu
from jax.sharding import Mesh, PartitionSpec as P

CLUSTERS = 64
SLOTS = 8
CAP = 512
LANES = 128
CORES = 2
CHUNKS = 4
GROUPS = CLUSTERS // CHUNKS
PART = GROUPS * SLOTS
TILES = 33
epsilon = 1e-06

VMEM = 32 * 1024 * 1024
NT = (((1,), (1,)), ((), ()))


def iota(shape, axis):
    return lax.broadcasted_iota(jnp.int32, shape, axis)


def as_bf16(mask):
    return jnp.where(mask, 1.0, 0.0).astype(jnp.bfloat16)


def pack_kernel(rows_hbm, cluster_hbm, order_hbm, out_ref, where_ref, rows_ref, ids_ref, sems):
    docs, width = rows_ref.shape
    cluster_copy = pltpu.make_async_copy(cluster_hbm, ids_ref.at[0], sems.at[0])
    order_copy = pltpu.make_async_copy(order_hbm, ids_ref.at[1], sems.at[1])
    rows_copy = pltpu.make_async_copy(rows_hbm, rows_ref, sems.at[2])
    cluster_copy.start()
    order_copy.start()
    rows_copy.start()
    before = as_bf16(iota((docs, docs), 0) < iota((docs, docs), 1))
    cluster_copy.wait()
    order_copy.wait()
    cluster = ids_ref[0]
    member = iota((CLUSTERS, docs), 0) == cluster
    count = jnp.dot(as_bf16(member), before, preferred_element_type=jnp.float32)
    position = jnp.sum(jnp.where(member, count, 0.0), axis=0, keepdims=True).astype(jnp.int32)
    chip = lax.axis_index("x") * lax.axis_size("zy") + lax.axis_index("zy")
    where_ref[0:1] = cluster
    where_ref[1:2] = chip // CHUNKS * SLOTS + (chip % CHUNKS * 2 + position) % SLOTS
    chunk = cluster % CHUNKS
    start = chunk * PART + cluster // CHUNKS * SLOTS
    line = iota((CHUNKS * PART, docs), 0)
    place = as_bf16(line == start + (chunk * 2 + position) % SLOTS)
    rank = ids_ref[1] - CAP
    high = (rank >> 4).astype(jnp.float32)
    low = (rank & 15).astype(jnp.float32)
    high_line = start + chunk * 2
    marks = jnp.where(line == high_line, high, jnp.where(line == high_line + 1, low, 0.0))
    marks = lax.dot_general(
        marks.astype(jnp.bfloat16),
        as_bf16(iota((LANES, docs), 0) == position),
        NT,
        preferred_element_type=jnp.float32,
    )
    rows_copy.wait()
    rows = rows_ref[...]
    squares = jnp.sum(rows * rows, axis=1, keepdims=True)
    unit = (rows * lax.rsqrt(squares + epsilon)).astype(jnp.bfloat16)
    line = iota((GROUPS, SLOTS, LANES), 1).astype(jnp.float32).astype(jnp.bfloat16)
    carried = None
    for at in range(CHUNKS):
        part = slice(at * PART, (at + 1) * PART)
        packed = jnp.dot(place[part], unit, preferred_element_type=jnp.float32)
        packed = packed.astype(jnp.bfloat16)
        mine = line >= jnp.asarray(at * 2, jnp.bfloat16)
        for lane in range(0, width, LANES):
            tile = packed[:, lane : lane + LANES].reshape(GROUPS, SLOTS, LANES)
            value = tile if carried is None else jnp.where(mine, tile, carried)
            out_ref[:, at * 8 + lane // LANES] = value
            carried = tile
        mark = marks[part].astype(jnp.bfloat16).reshape(GROUPS, SLOTS, LANES)
        carried = jnp.where(mine, mark, carried)
    out_ref[:, TILES - 1] = carried


def unfold(ref):
    slot = iota((GROUPS, SLOTS, LANES), 1)
    lane = iota((GROUPS, SLOTS, LANES), 2)
    rows, ranks = [], []
    for chunk in range(CHUNKS):
        turn = chunk * 2
        tiles = [ref[:, chunk * 8 + i] for i in range(9)]
        if chunk > 0:
            line = slot.astype(jnp.float32).astype(jnp.bfloat16)
            mine = line >= jnp.asarray(turn, jnp.bfloat16)
            data = [jnp.where(mine, x, y) for x, y in zip(tiles[:-1], tiles[1:])]
        else:
            data = tiles[:-1]
        rows.append(jnp.concatenate([x.reshape(PART, LANES) for x in data], axis=1))
        marks = tiles[-1].astype(jnp.float32)
        rank = marks[:, turn : turn + 1] * 16.0 + marks[:, turn + 1 : turn + 2]
        mine = lane == (slot - turn) % SLOTS
        rank = jnp.sum(jnp.where(mine, rank, 0.0), axis=2, keepdims=True)
        ranks.append(jnp.broadcast_to(rank, (GROUPS, SLOTS, LANES)).reshape(PART, LANES))
    return jnp.concatenate(rows, axis=0), jnp.concatenate(ranks, axis=0)


def best_of(keys, key_rank, queries_ref, rank_ref, first):
    step = 2 * LANES
    best = []
    for at in range(0, queries_ref.shape[1], step):
        similar = jnp.dot(
            keys, queries_ref[:, at : at + step], preferred_element_type=jnp.float32
        )
        for lane in range(0, step, LANES):
            allowed = key_rank < rank_ref[0:1, at + lane : at + lane + LANES]
            value = jnp.where(allowed, similar[:, lane : lane + LANES], -1.0)
            value = jnp.max(value.reshape(-1, 8, LANES), axis=0)
            best.append(jnp.maximum(value, first[:, at + lane : at + lane + LANES]))
    return best


def own_kernel(own_ref, queries_ref, rank_ref, best_ref):
    rows, ranks = unfold(own_ref)
    queries_ref[...] = rows.T
    rank_ref[...] = ranks.T[0:8]
    first = jnp.full(best_ref.shape, -1.0, jnp.float32)
    for at, best in enumerate(best_of(rows, ranks, queries_ref, rank_ref, first)):
        best_ref[:, at * LANES : (at + 1) * LANES] = best


def other_kernel(other_ref, queries_ref, rank_ref, first_ref, out_ref):
    rows, ranks = unfold(other_ref)
    best = best_of(rows, ranks, queries_ref, rank_ref, first_ref[...])
    lines = jnp.concatenate([jnp.max(x, axis=0, keepdims=True) for x in best])
    lines = jnp.concatenate([lines, lines])
    for at in range(0, CLUSTERS, 8):
        out_ref[at : at + 8] = lines


def unpack_kernel(best_ref, where_ref, out_ref):
    docs = where_ref.shape[1]
    best = jnp.concatenate([best_ref[...], jnp.zeros((LANES - CLUSTERS, LANES), jnp.float32)])
    cluster = jnp.broadcast_to(where_ref[0:1], (LANES, docs))
    by_cluster = jnp.take_along_axis(best.T, cluster, axis=1)
    wanted = iota((LANES, docs), 0) == where_ref[1:2]
    out_ref[...] = jnp.sum(jnp.where(wanted, by_cluster, 0.0), axis=0, keepdims=True)


def call(kernel, out_shape, flops, moved, **more):
    return pl.pallas_call(
        kernel,
        out_shape=out_shape,
        compiler_params=pltpu.CompilerParams(vmem_limit_bytes=VMEM),
        cost_estimate=pl.CostEstimate(flops=flops, bytes_accessed=moved, transcendentals=0),
        **more,
    )


def in_hbm(x):
    return pltpu.with_memory_space_constraint(x, pltpu.HBM)


def per_device(embeddings, cluster, order):
    docs, width = embeddings.shape
    slots = CLUSTERS * SLOTS
    shape = jax.ShapeDtypeStruct
    f32, bf16, i32 = jnp.float32, jnp.bfloat16, jnp.int32
    tiles = (GROUPS, TILES, 8, LANES)
    moved = CLUSTERS * (SLOTS * width + 2 * LANES) * 2
    packed, where = call(
        pack_kernel,
        (shape(tiles, bf16), shape((8, docs), i32)),
        2 * slots * docs * width,
        docs * width * 4 + moved,
        in_specs=[pl.BlockSpec(memory_space=pltpu.HBM)] * 3,
        scratch_shapes=[
            pltpu.VMEM((docs, width), f32),
            pltpu.VMEM((2, 1, docs), i32),
            pltpu.SemaphoreType.DMA((3,)),
        ],
    )(*(in_hbm(x) for x in (embeddings, cluster.reshape(1, docs), order.reshape(1, docs))))
    chunks = packed.reshape(CLUSTERS, TILES, 2, LANES)
    own = lax.all_to_all(chunks, ("x", "zy"), split_axis=0, concat_axis=0, tiled=True)
    other = lax.ppermute(own, "core", [(0, 1), (1, 0)])
    flops = 2 * slots * slots * width
    queries, rank, first = call(
        own_kernel,
        (shape((width, slots), bf16), shape((8, slots), f32), shape((8, slots), f32)),
        flops,
        2 * moved,
    )(own.reshape(tiles))
    best = call(other_kernel, shape((CLUSTERS, LANES), f32), flops, 2 * moved)(
        other.reshape(tiles), queries, rank, first
    )
    back = lax.all_to_all(best, ("x", "zy"), split_axis=0, concat_axis=0, tiled=True)
    result = call(unpack_kernel, shape((1, docs), f32), 0, CLUSTERS * LANES * 4)(back, where)
    return result.reshape(docs)


def solution(mesh):
    devices = mesh.devices.reshape(-1, CORES, mesh.shape["narrow"])
    chips = Mesh(devices, ("zy", "core", "x"))
    axes = ("zy", "core", "x")
    return jax.shard_map(
        per_device,
        mesh=chips,
        in_specs=(P(axes, None), P(axes), P(axes)),
        out_specs=P(axes),
        check_vma=False,
    )
```

```python
import jax
import jax.numpy as jnp
from jax import lax
from jax.experimental import pallas as pl
from jax.experimental.pallas import tpu as pltpu
from jax.sharding import Mesh, PartitionSpec as P

CLUSTERS = 64
SLOTS = 8
CAP = 512
LANES = 128
CORES = 2
CHUNKS = 4
GROUPS = CLUSTERS // CHUNKS
PART = GROUPS * SLOTS
TILES = 33
epsilon = 1e-06

VMEM = 32 * 1024 * 1024
NT = (((1,), (1,)), ((), ()))


def iota(shape, axis):
    return lax.broadcasted_iota(jnp.int32, shape, axis)


def as_bf16(mask):
    return jnp.where(mask, 1.0, 0.0).astype(jnp.bfloat16)


def pack_kernel(rows_hbm, cluster_hbm, order_hbm, out_ref, where_ref, rows_ref, ids_ref, sems):
    docs, width = rows_ref.shape
    cluster_copy = pltpu.make_async_copy(cluster_hbm, ids_ref.at[0], sems.at[0])
    order_copy = pltpu.make_async_copy(order_hbm, ids_ref.at[1], sems.at[1])
    rows_copy = pltpu.make_async_copy(rows_hbm, rows_ref, sems.at[2])
    cluster_copy.start()
    order_copy.start()
    rows_copy.start()
    before = as_bf16(iota((docs, docs), 0) < iota((docs, docs), 1))
    cluster_copy.wait()
    order_copy.wait()
    cluster = ids_ref[0]
    member = iota((CLUSTERS, docs), 0) == cluster
    count = jnp.dot(as_bf16(member), before, preferred_element_type=jnp.float32)
    position = jnp.sum(jnp.where(member, count, 0.0), axis=0, keepdims=True).astype(jnp.int32)
    chip = lax.axis_index("x") * lax.axis_size("zy") + lax.axis_index("zy")
    where_ref[0:1] = cluster
    where_ref[1:2] = chip // CHUNKS * SLOTS + (chip % CHUNKS * 2 + position) % SLOTS
    chunk = cluster % CHUNKS
    start = chunk * PART + cluster // CHUNKS * SLOTS
    line = iota((CHUNKS * PART, docs), 0)
    place = as_bf16(line == start + (chunk * 2 + position) % SLOTS)
    rank = ids_ref[1] - CAP
    high = (rank >> 4).astype(jnp.float32)
    low = (rank & 15).astype(jnp.float32)
    high_line = start + chunk * 2
    marks = jnp.where(line == high_line, high, jnp.where(line == high_line + 1, low, 0.0))
    marks = lax.dot_general(
        marks.astype(jnp.bfloat16),
        as_bf16(iota((LANES, docs), 0) == position),
        NT,
        preferred_element_type=jnp.float32,
    )
    rows_copy.wait()
    rows = rows_ref[...]
    squares = jnp.sum(rows * rows, axis=1, keepdims=True)
    unit = (rows * lax.rsqrt(squares + epsilon)).astype(jnp.bfloat16)
    line = iota((GROUPS, SLOTS, LANES), 1).astype(jnp.float32).astype(jnp.bfloat16)
    carried = None
    for at in range(CHUNKS):
        part = slice(at * PART, (at + 1) * PART)
        packed = jnp.dot(place[part], unit, preferred_element_type=jnp.float32)
        packed = packed.astype(jnp.bfloat16)
        mine = line >= jnp.asarray(at * 2, jnp.bfloat16)
        for lane in range(0, width, LANES):
            tile = packed[:, lane : lane + LANES].reshape(GROUPS, SLOTS, LANES)
            value = tile if carried is None else jnp.where(mine, tile, carried)
            out_ref[:, at * 8 + lane // LANES] = value
            carried = tile
        mark = marks[part].astype(jnp.bfloat16).reshape(GROUPS, SLOTS, LANES)
        carried = jnp.where(mine, mark, carried)
    out_ref[:, TILES - 1] = carried


def unfold(ref):
    slot = iota((GROUPS, SLOTS, LANES), 1)
    lane = iota((GROUPS, SLOTS, LANES), 2)
    rows, ranks = [], []
    for chunk in range(CHUNKS):
        turn = chunk * 2
        tiles = [ref[:, chunk * 8 + i] for i in range(9)]
        if chunk > 0:
            line = slot.astype(jnp.float32).astype(jnp.bfloat16)
            mine = line >= jnp.asarray(turn, jnp.bfloat16)
            data = [jnp.where(mine, x, y) for x, y in zip(tiles[:-1], tiles[1:])]
        else:
            data = tiles[:-1]
        rows.append(jnp.concatenate([x.reshape(PART, LANES) for x in data], axis=1))
        marks = tiles[-1].astype(jnp.float32)
        rank = marks[:, turn : turn + 1] * 16.0 + marks[:, turn + 1 : turn + 2]
        mine = lane == (slot - turn) % SLOTS
        rank = jnp.sum(jnp.where(mine, rank, 0.0), axis=2, keepdims=True)
        ranks.append(jnp.broadcast_to(rank, (GROUPS, SLOTS, LANES)).reshape(PART, LANES))
    return jnp.concatenate(rows, axis=0), jnp.concatenate(ranks, axis=0)


def largest(values):
    return jnp.max(values.reshape(-1, 8, values.shape[1]), axis=0)


def similarities(keys, queries_ref):
    step = 2 * LANES
    for at in range(0, queries_ref.shape[1], step):
        similar = jnp.dot(
            keys, queries_ref[:, at : at + step], preferred_element_type=jnp.float32
        )
        for lane in range(0, step, LANES):
            yield at + lane, similar[:, lane : lane + LANES]


def cross_kernel(own_ref, other_ref, queries_ref, rank_ref, cross_ref, away_ref):
    rows, ranks = unfold(own_ref)
    queries_ref[...] = rows.T
    rank_ref[...] = ranks.T[0:8]
    keys, key_rank = unfold(other_ref)
    away = jnp.full(key_rank.shape, -1.0, jnp.float32)
    for at, similar in similarities(keys, queries_ref):
        rank = rank_ref[0:1, at : at + LANES]
        cross_ref[:, at : at + LANES] = largest(jnp.where(key_rank < rank, similar, -1.0))
        away = jnp.maximum(away, jnp.where(rank < key_rank, similar, -1.0))
    away_ref[...] = largest(away.T)


def own_kernel(own_ref, queries_ref, rank_ref, best_ref):
    keys, key_rank = unfold(own_ref)
    for at, similar in similarities(keys, queries_ref):
        allowed = key_rank < rank_ref[0:1, at : at + LANES]
        best_ref[:, at : at + LANES] = largest(jnp.where(allowed, similar, -1.0))


def merge_kernel(best_ref, cross_ref, away_ref, out_ref):
    first = lax.axis_index("core") == 0
    best = jnp.maximum(best_ref[...], jnp.where(first, cross_ref[...], away_ref[...]))
    best = jnp.max(best, axis=0, keepdims=True)
    lines = [best[:, at : at + LANES] for at in range(0, best.shape[1], LANES)]
    lines = jnp.concatenate(lines + lines)
    for at in range(0, CLUSTERS, 8):
        out_ref[at : at + 8] = lines


def unpack_kernel(best_ref, where_ref, out_ref):
    docs = where_ref.shape[1]
    best = jnp.concatenate([best_ref[...], jnp.zeros((LANES - CLUSTERS, LANES), jnp.float32)])
    cluster = jnp.broadcast_to(where_ref[0:1], (LANES, docs))
    by_cluster = jnp.take_along_axis(best.T, cluster, axis=1)
    wanted = iota((LANES, docs), 0) == where_ref[1:2]
    out_ref[...] = jnp.sum(jnp.where(wanted, by_cluster, 0.0), axis=0, keepdims=True)


def call(kernel, out_shape, flops, moved, **more):
    return pl.pallas_call(
        kernel,
        out_shape=out_shape,
        compiler_params=pltpu.CompilerParams(vmem_limit_bytes=VMEM),
        cost_estimate=pl.CostEstimate(flops=flops, bytes_accessed=moved, transcendentals=0),
        **more,
    )


def in_hbm(x):
    return pltpu.with_memory_space_constraint(x, pltpu.HBM)


def per_device(embeddings, cluster, order):
    docs, width = embeddings.shape
    slots = CLUSTERS * SLOTS
    shape = jax.ShapeDtypeStruct
    f32, bf16, i32 = jnp.float32, jnp.bfloat16, jnp.int32
    tiles = (GROUPS, TILES, 8, LANES)
    moved = CLUSTERS * (SLOTS * width + 2 * LANES) * 2
    packed, where = call(
        pack_kernel,
        (shape(tiles, bf16), shape((8, docs), i32)),
        2 * slots * docs * width,
        docs * width * 4 + moved,
        in_specs=[pl.BlockSpec(memory_space=pltpu.HBM)] * 3,
        scratch_shapes=[
            pltpu.VMEM((docs, width), f32),
            pltpu.VMEM((2, 1, docs), i32),
            pltpu.SemaphoreType.DMA((3,)),
        ],
    )(*(in_hbm(x) for x in (embeddings, cluster.reshape(1, docs), order.reshape(1, docs))))
    chunks = packed.reshape(CLUSTERS, TILES, 2, LANES)

    def exchange(sent, ready):
        return lax.all_to_all(sent, ("x", "zy"), split_axis=0, concat_axis=0, tiled=True)

    def keep(sent, ready):
        return ready

    core = lax.axis_index("core")
    early = lax.cond(core == 1, exchange, keep, chunks, chunks)
    other = lax.ppermute(early, "core", [(1, 0)])
    own = lax.cond(core == 0, exchange, keep, chunks, early).reshape(tiles)
    flops = 2 * slots * slots * width
    line = shape((8, slots), f32)
    queries, rank, cross, away = call(
        cross_kernel, (shape((width, slots), bf16), line, line, line), flops, 3 * moved
    )(own, other.reshape(tiles))
    away = lax.ppermute(away, "core", [(0, 1)])
    best = call(own_kernel, line, flops, 2 * moved)(own, queries, rank)
    best = call(merge_kernel, shape((CLUSTERS, LANES), f32), 0, CLUSTERS * LANES * 4)(
        best, cross, away
    )
    back = lax.all_to_all(best, ("x", "zy"), split_axis=0, concat_axis=0, tiled=True)
    result = call(unpack_kernel, shape((1, docs), f32), 0, CLUSTERS * LANES * 4)(back, where)
    return result.reshape(docs)


def solution(mesh):
    devices = mesh.devices.reshape(-1, CORES, mesh.shape["narrow"])
    chips = Mesh(devices, ("zy", "core", "x"))
    axes = ("zy", "core", "x")
    return jax.shard_map(
        per_device,
        mesh=chips,
        in_specs=(P(axes, None), P(axes), P(axes)),
        out_specs=P(axes),
        check_vma=False,
    )
```

```python
import jax
import jax.numpy as jnp
from jax import lax
from jax.experimental import pallas as pl
from jax.experimental.pallas import tpu as pltpu
from jax.sharding import Mesh, PartitionSpec as P

CLUSTERS = 64
SLOTS = 8
CAP = 512
LANES = 128
CORES = 2
CHUNKS = 4
GROUPS = CLUSTERS // CHUNKS
PART = GROUPS * SLOTS
TILES = 33
epsilon = 1e-06

VMEM = 32 * 1024 * 1024
NT = (((1,), (1,)), ((), ()))


def iota(shape, axis):
    return lax.broadcasted_iota(jnp.int32, shape, axis)


def as_bf16(mask):
    return jnp.where(mask, 1.0, 0.0).astype(jnp.bfloat16)


def pack_kernel(rows_hbm, cluster_hbm, order_hbm, out_ref, where_ref, rows_ref, ids_ref, sems):
    docs, width = rows_ref.shape
    cluster_copy = pltpu.make_async_copy(cluster_hbm, ids_ref.at[0], sems.at[0])
    order_copy = pltpu.make_async_copy(order_hbm, ids_ref.at[1], sems.at[1])
    rows_copy = pltpu.make_async_copy(rows_hbm, rows_ref, sems.at[2])
    cluster_copy.start()
    order_copy.start()
    rows_copy.start()
    before = as_bf16(iota((docs, docs), 0) < iota((docs, docs), 1))
    cluster_copy.wait()
    order_copy.wait()
    cluster = ids_ref[0]
    member = iota((CLUSTERS, docs), 0) == cluster
    count = jnp.dot(as_bf16(member), before, preferred_element_type=jnp.float32)
    position = jnp.sum(jnp.where(member, count, 0.0), axis=0, keepdims=True).astype(jnp.int32)
    chip = lax.axis_index("x") * lax.axis_size("zy") + lax.axis_index("zy")
    where_ref[0:1] = cluster
    where_ref[1:2] = chip // CHUNKS * SLOTS + (chip % CHUNKS * 2 + position) % SLOTS
    chunk = cluster % CHUNKS
    start = chunk * PART + cluster // CHUNKS * SLOTS
    line = iota((CHUNKS * PART, docs), 0)
    place = as_bf16(line == start + (chunk * 2 + position) % SLOTS)
    rank = ids_ref[1] - CAP
    high = (rank >> 4).astype(jnp.float32)
    low = (rank & 15).astype(jnp.float32)
    high_line = start + chunk * 2
    marks = jnp.where(line == high_line, high, jnp.where(line == high_line + 1, low, 0.0))
    marks = lax.dot_general(
        marks.astype(jnp.bfloat16),
        as_bf16(iota((LANES, docs), 0) == position),
        NT,
        preferred_element_type=jnp.float32,
    )
    rows_copy.wait()
    rows = rows_ref[...]
    squares = jnp.sum(rows * rows, axis=1, keepdims=True)
    unit = (rows * lax.rsqrt(squares + epsilon)).astype(jnp.bfloat16)
    line = iota((GROUPS, SLOTS, LANES), 1).astype(jnp.float32).astype(jnp.bfloat16)
    carried = None
    for at in range(CHUNKS):
        part = slice(at * PART, (at + 1) * PART)
        packed = jnp.dot(place[part], unit, preferred_element_type=jnp.float32)
        packed = packed.astype(jnp.bfloat16)
        mine = line >= jnp.asarray(at * 2, jnp.bfloat16)
        for lane in range(0, width, LANES):
            tile = packed[:, lane : lane + LANES].reshape(GROUPS, SLOTS, LANES)
            value = tile if carried is None else jnp.where(mine, tile, carried)
            out_ref[:, at * 8 + lane // LANES] = value
            carried = tile
        mark = marks[part].astype(jnp.bfloat16).reshape(GROUPS, SLOTS, LANES)
        carried = jnp.where(mine, mark, carried)
    out_ref[:, TILES - 1] = carried


def unfold(ref):
    slot = iota((GROUPS, SLOTS, LANES), 1)
    lane = iota((GROUPS, SLOTS, LANES), 2)
    rows, ranks = [], []
    for chunk in range(CHUNKS):
        turn = chunk * 2
        tiles = [ref[:, chunk * 8 + i] for i in range(9)]
        if chunk > 0:
            line = slot.astype(jnp.float32).astype(jnp.bfloat16)
            mine = line >= jnp.asarray(turn, jnp.bfloat16)
            data = [jnp.where(mine, x, y) for x, y in zip(tiles[:-1], tiles[1:])]
        else:
            data = tiles[:-1]
        rows.append(jnp.concatenate([x.reshape(PART, LANES) for x in data], axis=1))
        marks = tiles[-1].astype(jnp.float32)
        rank = marks[:, turn : turn + 1] * 16.0 + marks[:, turn + 1 : turn + 2]
        mine = lane == (slot - turn) % SLOTS
        rank = jnp.sum(jnp.where(mine, rank, 0.0), axis=2, keepdims=True)
        ranks.append(jnp.broadcast_to(rank, (GROUPS, SLOTS, LANES)).reshape(PART, LANES))
    return jnp.concatenate(rows, axis=0), jnp.concatenate(ranks, axis=0)


def largest(values):
    return jnp.max(values.reshape(-1, 8, values.shape[1]), axis=0)


def similarities(keys, queries_ref):
    step = 2 * LANES
    for at in range(0, queries_ref.shape[1], step):
        similar = jnp.dot(
            keys, queries_ref[:, at : at + step], preferred_element_type=jnp.float32
        )
        for lane in range(0, step, LANES):
            yield at + lane, similar[:, lane : lane + LANES]


def maxima(keys, key_rank, queries_ref, rank_ref):
    for at, similar in similarities(keys, queries_ref):
        allowed = key_rank < rank_ref[0:1, at : at + LANES]
        yield at, largest(jnp.where(allowed, similar, -1.0))


def first_kernel(early_ref, late_ref, other_ref, queries_ref, rank_ref, best_ref, away_ref):
    core = lax.axis_index("core")

    def turn(rows, ranks):
        queries_ref[...] = rows.T
        rank_ref[...] = ranks.T[0:8]

    @pl.when(core == 0)
    def _():
        turn(*unfold(late_ref))
        keys, key_rank = unfold(other_ref)
        away = jnp.full(key_rank.shape, -1.0, jnp.float32)
        for at, similar in similarities(keys, queries_ref):
            rank = rank_ref[0:1, at : at + LANES]
            best_ref[:, at : at + LANES] = largest(jnp.where(key_rank < rank, similar, -1.0))
            away = jnp.maximum(away, jnp.where(rank < key_rank, similar, -1.0))
        away_ref[...] = largest(away.T)

    @pl.when(core != 0)
    def _():
        rows, ranks = unfold(early_ref)
        turn(rows, ranks)
        for at, best in maxima(rows, ranks, queries_ref, rank_ref):
            best_ref[:, at : at + LANES] = best
        away_ref[...] = jnp.full(away_ref.shape, -1.0, jnp.float32)


def second_kernel(late_ref, queries_ref, rank_ref, first_ref, best_ref):
    core = lax.axis_index("core")

    @pl.when(core == 0)
    def _():
        for at, best in maxima(*unfold(late_ref), queries_ref, rank_ref):
            best_ref[:, at : at + LANES] = jnp.maximum(best, first_ref[:, at : at + LANES])

    @pl.when(core != 0)
    def _():
        best_ref[...] = first_ref[...]


def merge_kernel(best_ref, away_ref, out_ref):
    away = jnp.where(lax.axis_index("core") == 0, -1.0, away_ref[...])
    best = jnp.max(jnp.maximum(best_ref[...], away), axis=0, keepdims=True)
    lines = [best[:, at : at + LANES] for at in range(0, best.shape[1], LANES)]
    lines = jnp.concatenate(lines + lines)
    for at in range(0, CLUSTERS, 8):
        out_ref[at : at + 8] = lines


def unpack_kernel(best_ref, where_ref, out_ref):
    docs = where_ref.shape[1]
    best = jnp.concatenate([best_ref[...], jnp.zeros((LANES - CLUSTERS, LANES), jnp.float32)])
    cluster = jnp.broadcast_to(where_ref[0:1], (LANES, docs))
    by_cluster = jnp.take_along_axis(best.T, cluster, axis=1)
    wanted = iota((LANES, docs), 0) == where_ref[1:2]
    out_ref[...] = jnp.sum(jnp.where(wanted, by_cluster, 0.0), axis=0, keepdims=True)


def call(kernel, out_shape, flops, moved, **more):
    return pl.pallas_call(
        kernel,
        out_shape=out_shape,
        compiler_params=pltpu.CompilerParams(vmem_limit_bytes=VMEM),
        cost_estimate=pl.CostEstimate(flops=flops, bytes_accessed=moved, transcendentals=0),
        **more,
    )


def in_hbm(x):
    return pltpu.with_memory_space_constraint(x, pltpu.HBM)


def per_device(embeddings, cluster, order):
    docs, width = embeddings.shape
    slots = CLUSTERS * SLOTS
    shape = jax.ShapeDtypeStruct
    f32, bf16, i32 = jnp.float32, jnp.bfloat16, jnp.int32
    tiles = (GROUPS, TILES, 8, LANES)
    moved = CLUSTERS * (SLOTS * width + 2 * LANES) * 2
    packed, where = call(
        pack_kernel,
        (shape(tiles, bf16), shape((8, docs), i32)),
        2 * slots * docs * width,
        docs * width * 4 + moved,
        in_specs=[pl.BlockSpec(memory_space=pltpu.HBM)] * 3,
        scratch_shapes=[
            pltpu.VMEM((docs, width), f32),
            pltpu.VMEM((2, 1, docs), i32),
            pltpu.SemaphoreType.DMA((3,)),
        ],
    )(*(in_hbm(x) for x in (embeddings, cluster.reshape(1, docs), order.reshape(1, docs))))
    chunks = packed.reshape(CLUSTERS, TILES, 2, LANES)

    def exchange(sent):
        return lax.all_to_all(sent, ("x", "zy"), split_axis=0, concat_axis=0, tiled=True)

    def keep(sent):
        return sent

    core = lax.axis_index("core")
    early = lax.cond(core == 1, exchange, keep, chunks)
    other = lax.ppermute(early, "core", [(1, 0)]).reshape(tiles)
    late = lax.cond(core == 0, exchange, keep, chunks).reshape(tiles)
    early = early.reshape(tiles)
    flops = 2 * slots * slots * width
    line = shape((8, slots), f32)
    queries, rank, first, away = call(
        first_kernel, (shape((width, slots), bf16), line, line, line), flops, 3 * moved
    )(early, late, other)
    away = lax.ppermute(away, "core", [(0, 1), (1, 0)])
    best = call(second_kernel, line, flops, 2 * moved)(late, queries, rank, first)
    best = call(merge_kernel, shape((CLUSTERS, LANES), f32), 0, CLUSTERS * LANES * 4)(best, away)
    back = lax.all_to_all(best, ("x", "zy"), split_axis=0, concat_axis=0, tiled=True)
    result = call(unpack_kernel, shape((1, docs), f32), 0, CLUSTERS * LANES * 4)(back, where)
    return result.reshape(docs)


def solution(mesh):
    devices = mesh.devices.reshape(-1, CORES, mesh.shape["narrow"])
    chips = Mesh(devices, ("zy", "core", "x"))
    axes = ("zy", "core", "x")
    return jax.shard_map(
        per_device,
        mesh=chips,
        in_specs=(P(axes, None), P(axes), P(axes)),
        out_specs=P(axes),
        check_vma=False,
    )
```

```python
import jax
import jax.numpy as jnp
from jax import lax
from jax.experimental import pallas as pl
from jax.experimental.pallas import tpu as pltpu
from jax.sharding import Mesh, PartitionSpec as P

CLUSTERS = 64
SLOTS = 8
CAP = 512
LANES = 128
CORES = 2
CHUNKS = 4
GROUPS = CLUSTERS // CHUNKS
PART = GROUPS * SLOTS
TILES = 33
MARKS = 16
epsilon = 1e-06

VMEM = 32 * 1024 * 1024
NT = (((1,), (1,)), ((), ()))


def iota(shape, axis):
    return lax.broadcasted_iota(jnp.int32, shape, axis)


def as_bf16(mask):
    return jnp.where(mask, 1.0, 0.0).astype(jnp.bfloat16)


def pack_kernel(rows_hbm, cluster_hbm, order_hbm, out_ref, where_ref, rows_ref, ids_ref, sems):
    docs, width = rows_ref.shape
    cluster_copy = pltpu.make_async_copy(cluster_hbm, ids_ref.at[0], sems.at[0])
    order_copy = pltpu.make_async_copy(order_hbm, ids_ref.at[1], sems.at[1])
    rows_copy = pltpu.make_async_copy(rows_hbm, rows_ref, sems.at[2])
    cluster_copy.start()
    order_copy.start()
    rows_copy.start()
    before = as_bf16(iota((docs, docs), 0) < iota((docs, docs), 1))
    cluster_copy.wait()
    order_copy.wait()
    cluster = ids_ref[0]
    member = iota((CLUSTERS, docs), 0) == cluster
    count = jnp.dot(as_bf16(member), before, preferred_element_type=jnp.float32)
    position = jnp.sum(jnp.where(member, count, 0.0), axis=0, keepdims=True).astype(jnp.int32)
    chip = lax.axis_index("x") * lax.axis_size("zy") + lax.axis_index("zy")
    where_ref[0:1] = cluster
    where_ref[1:2] = chip // CHUNKS * SLOTS + (chip % CHUNKS * 2 + position) % SLOTS
    chunk = cluster % CHUNKS
    start = chunk * PART + cluster // CHUNKS * SLOTS
    line = iota((CHUNKS * PART, docs), 0)
    place = as_bf16(line == start + (chunk * 2 + position) % SLOTS)
    rank = ids_ref[1] - CAP
    high = (rank >> 4).astype(jnp.float32)
    low = (rank & 15).astype(jnp.float32)
    high_line = start + chunk * 2
    marks = jnp.where(line == high_line, high, jnp.where(line == high_line + 1, low, 0.0))
    marks = lax.dot_general(
        marks.astype(jnp.bfloat16),
        as_bf16(iota((LANES, docs), 0) == position),
        NT,
        preferred_element_type=jnp.float32,
    )
    rows_copy.wait()
    rows = rows_ref[...]
    squares = jnp.sum(rows * rows, axis=1, keepdims=True)
    unit = (rows * lax.rsqrt(squares + epsilon)).astype(jnp.bfloat16)
    line = iota((GROUPS, SLOTS, LANES), 1).astype(jnp.float32).astype(jnp.bfloat16)
    carried = None
    for at in range(CHUNKS):
        part = slice(at * PART, (at + 1) * PART)
        packed = jnp.dot(place[part], unit, preferred_element_type=jnp.float32)
        packed = packed.astype(jnp.bfloat16)
        mine = line >= jnp.asarray(at * 2, jnp.bfloat16)
        for lane in range(0, width, LANES):
            tile = packed[:, lane : lane + LANES].reshape(GROUPS, SLOTS, LANES)
            value = tile if carried is None else jnp.where(mine, tile, carried)
            out_ref[:, at * 8 + lane // LANES] = value
            carried = tile
        mark = marks[part].astype(jnp.bfloat16).reshape(GROUPS, SLOTS, LANES)
        carried = jnp.where(mine, mark, carried)
    out_ref[:, TILES - 1] = carried


def unfold(ref):
    slot = iota((GROUPS, SLOTS, LANES), 1)
    lane = iota((GROUPS, SLOTS, LANES), 2)
    rows, ranks = [], []
    for chunk in range(CHUNKS):
        turn = chunk * 2
        tiles = [ref[:, chunk * 8 + i] for i in range(9)]
        if chunk > 0:
            line = slot.astype(jnp.float32).astype(jnp.bfloat16)
            mine = line >= jnp.asarray(turn, jnp.bfloat16)
            data = [jnp.where(mine, x, y) for x, y in zip(tiles[:-1], tiles[1:])]
        else:
            data = tiles[:-1]
        rows.append(jnp.concatenate([x.reshape(PART, LANES) for x in data], axis=1))
        marks = tiles[-1].astype(jnp.float32)
        rank = marks[:, turn : turn + 1] * 16.0 + marks[:, turn + 1 : turn + 2]
        mine = lane == (slot - turn) % SLOTS
        rank = jnp.sum(jnp.where(mine, rank, 0.0), axis=2, keepdims=True)
        ranks.append(jnp.broadcast_to(rank, (GROUPS, SLOTS, LANES)).reshape(PART, LANES))
    return jnp.concatenate(rows, axis=0), jnp.concatenate(ranks, axis=0)


def largest(values):
    return jnp.max(values.reshape(-1, 8, values.shape[1]), axis=0)


def similarities(keys, queries_ref):
    step = 2 * LANES
    for at in range(0, queries_ref.shape[1], step):
        similar = jnp.dot(
            keys, queries_ref[: keys.shape[1], at : at + step], preferred_element_type=jnp.float32
        )
        for lane in range(0, step, LANES):
            yield at + lane, similar[:, lane : lane + LANES]


def maxima(keys, key_rank, queries_ref, query_rank):
    for at, similar in similarities(keys, queries_ref):
        allowed = key_rank < query_rank[0:1, at : at + LANES]
        yield at, largest(jnp.where(allowed, similar, -1.0))


def turn_kernel(early_ref, turned_ref, best_ref):
    core = lax.axis_index("core")
    width = turned_ref.shape[0] - MARKS

    @pl.when(core == 0)
    def _():
        best_ref[...] = jnp.full(best_ref.shape, -1.0, jnp.float32)

    @pl.when(core != 0)
    def _():
        rows, ranks = unfold(early_ref)
        turned_ref[:width] = rows.T
        rank = ranks.T[0:MARKS]
        high = jnp.floor(rank * 0.0625)
        parts = jnp.where(iota(rank.shape, 0) == 0, high, rank - high * 16.0)
        turned_ref[width:] = parts.astype(jnp.bfloat16)
        for at, best in maxima(rows, ranks, turned_ref, rank):
            best_ref[:, at : at + LANES] = best


def first_kernel(late_ref, other_ref, cross_ref, away_ref):
    core = lax.axis_index("core")
    width = other_ref.shape[0] - MARKS

    @pl.when(core == 0)
    def _():
        rows, ranks = unfold(late_ref)
        marks = other_ref[width:].astype(jnp.float32)
        other_rank = marks[0:1] * 16.0 + marks[1:2]
        best = jnp.full(ranks.shape, -1.0, jnp.float32)
        for at, similar in similarities(rows, other_ref):
            rank = other_rank[:, at : at + LANES]
            away_ref[:, at : at + LANES] = largest(jnp.where(ranks < rank, similar, -1.0))
            best = jnp.maximum(best, jnp.where(rank < ranks, similar, -1.0))
        cross_ref[...] = best

    @pl.when(core != 0)
    def _():
        away_ref[...] = jnp.full(away_ref.shape, -1.0, jnp.float32)
        cross_ref[...] = jnp.full(cross_ref.shape, -1.0, jnp.float32)


def second_kernel(late_ref, first_ref, cross_ref, best_ref, queries_ref):
    core = lax.axis_index("core")

    @pl.when(core == 0)
    def _():
        rows, ranks = unfold(late_ref)
        queries_ref[...] = rows.T
        cross = largest(cross_ref[...].T)
        for at, best in maxima(rows, ranks, queries_ref, ranks.T[0:8]):
            best_ref[:, at : at + LANES] = jnp.maximum(best, cross[:, at : at + LANES])

    @pl.when(core != 0)
    def _():
        best_ref[...] = first_ref[...]


def merge_kernel(best_ref, away_ref, out_ref):
    away = jnp.where(lax.axis_index("core") == 0, -1.0, away_ref[...])
    best = jnp.max(jnp.maximum(best_ref[...], away), axis=0, keepdims=True)
    lines = [best[:, at : at + LANES] for at in range(0, best.shape[1], LANES)]
    lines = jnp.concatenate(lines + lines)
    for at in range(0, CLUSTERS, 8):
        out_ref[at : at + 8] = lines


def unpack_kernel(best_ref, where_ref, out_ref):
    docs = where_ref.shape[1]
    best = jnp.concatenate([best_ref[...], jnp.zeros((LANES - CLUSTERS, LANES), jnp.float32)])
    cluster = jnp.broadcast_to(where_ref[0:1], (LANES, docs))
    by_cluster = jnp.take_along_axis(best.T, cluster, axis=1)
    wanted = iota((LANES, docs), 0) == where_ref[1:2]
    out_ref[...] = jnp.sum(jnp.where(wanted, by_cluster, 0.0), axis=0, keepdims=True)


def call(kernel, out_shape, flops, moved, **more):
    return pl.pallas_call(
        kernel,
        out_shape=out_shape,
        compiler_params=pltpu.CompilerParams(vmem_limit_bytes=VMEM),
        cost_estimate=pl.CostEstimate(flops=flops, bytes_accessed=moved, transcendentals=0),
        **more,
    )


def in_hbm(x):
    return pltpu.with_memory_space_constraint(x, pltpu.HBM)


def per_device(embeddings, cluster, order):
    docs, width = embeddings.shape
    slots = CLUSTERS * SLOTS
    shape = jax.ShapeDtypeStruct
    f32, bf16, i32 = jnp.float32, jnp.bfloat16, jnp.int32
    tiles = (GROUPS, TILES, 8, LANES)
    moved = CLUSTERS * (SLOTS * width + 2 * LANES) * 2
    packed, where = call(
        pack_kernel,
        (shape(tiles, bf16), shape((8, docs), i32)),
        2 * slots * docs * width,
        docs * width * 4 + moved,
        in_specs=[pl.BlockSpec(memory_space=pltpu.HBM)] * 3,
        scratch_shapes=[
            pltpu.VMEM((docs, width), f32),
            pltpu.VMEM((2, 1, docs), i32),
            pltpu.SemaphoreType.DMA((3,)),
        ],
    )(*(in_hbm(x) for x in (embeddings, cluster.reshape(1, docs), order.reshape(1, docs))))
    chunks = packed.reshape(CLUSTERS, TILES, 2, LANES)

    def exchange(sent):
        return lax.all_to_all(sent, ("x", "zy"), split_axis=0, concat_axis=0, tiled=True)

    def keep(sent):
        return sent

    core = lax.axis_index("core")
    early = lax.cond(core == 1, exchange, keep, chunks)
    late = lax.cond(core == 0, exchange, keep, chunks).reshape(tiles)
    flops = 2 * slots * slots * width
    line = shape((8, slots), f32)
    turned, first = call(
        turn_kernel,
        (pltpu.VMEM((width + MARKS, slots), bf16), pltpu.VMEM((8, slots), f32)),
        flops,
        2 * moved,
    )(pltpu.with_memory_space_constraint(early.reshape(tiles), pltpu.VMEM))
    other = lax.ppermute(turned, "core", [(1, 0)])
    cross, away = call(first_kernel, (shape((slots, LANES), f32), line), flops, 2 * moved)(
        late, other
    )
    away = lax.ppermute(away, "core", [(0, 1), (1, 0)])
    best = call(
        second_kernel,
        line,
        flops,
        2 * moved,
        scratch_shapes=[pltpu.VMEM((width, slots), bf16)],
    )(late, first, cross)
    best = call(merge_kernel, shape((CLUSTERS, LANES), f32), 0, CLUSTERS * LANES * 4)(best, away)
    back = lax.all_to_all(best, ("x", "zy"), split_axis=0, concat_axis=0, tiled=True)
    result = call(unpack_kernel, shape((1, docs), f32), 0, CLUSTERS * LANES * 4)(back, where)
    return result.reshape(docs)


def solution(mesh):
    devices = mesh.devices.reshape(-1, CORES, mesh.shape["narrow"])
    chips = Mesh(devices, ("zy", "core", "x"))
    axes = ("zy", "core", "x")
    return jax.shard_map(
        per_device,
        mesh=chips,
        in_specs=(P(axes, None), P(axes), P(axes)),
        out_specs=P(axes),
        check_vma=False,
    )
```

```python
import jax
import jax.numpy as jnp
from jax import lax
from jax.experimental import pallas as pl
from jax.experimental.pallas import tpu as pltpu
from jax.sharding import Mesh, PartitionSpec as P

CLUSTERS = 64
SLOTS = 8
CAP = 512
LANES = 128
CORES = 2
CHUNKS = 4
GROUPS = CLUSTERS // CHUNKS
PART = GROUPS * SLOTS
TILES = 33
MARKS = 16
epsilon = 1e-06

VMEM = 32 * 1024 * 1024
NT = (((1,), (1,)), ((), ()))


def iota(shape, axis):
    return lax.broadcasted_iota(jnp.int32, shape, axis)


def as_bf16(mask):
    return jnp.where(mask, 1.0, 0.0).astype(jnp.bfloat16)


def pack_kernel(rows_hbm, cluster_hbm, order_hbm, out_ref, where_ref, rows_ref, ids_ref, sems):
    docs, width = rows_ref.shape
    cluster_copy = pltpu.make_async_copy(cluster_hbm, ids_ref.at[0], sems.at[0])
    order_copy = pltpu.make_async_copy(order_hbm, ids_ref.at[1], sems.at[1])
    rows_copy = pltpu.make_async_copy(rows_hbm, rows_ref, sems.at[2])
    cluster_copy.start()
    order_copy.start()
    rows_copy.start()
    before = as_bf16(iota((docs, docs), 0) < iota((docs, docs), 1))
    cluster_copy.wait()
    order_copy.wait()
    cluster = ids_ref[0]
    member = iota((CLUSTERS, docs), 0) == cluster
    count = jnp.dot(as_bf16(member), before, preferred_element_type=jnp.float32)
    position = jnp.sum(jnp.where(member, count, 0.0), axis=0, keepdims=True).astype(jnp.int32)
    chip = lax.axis_index("x") * lax.axis_size("zy") + lax.axis_index("zy")
    where_ref[0:1] = cluster
    where_ref[1:2] = chip // CHUNKS * SLOTS + (chip % CHUNKS * 2 + position) % SLOTS
    chunk = cluster % CHUNKS
    start = chunk * PART + cluster // CHUNKS * SLOTS
    line = iota((CHUNKS * PART, docs), 0)
    place = as_bf16(line == start + (chunk * 2 + position) % SLOTS)
    rank = ids_ref[1] - CAP
    high = (rank >> 4).astype(jnp.float32)
    low = (rank & 15).astype(jnp.float32)
    high_line = start + chunk * 2
    marks = jnp.where(line == high_line, high, jnp.where(line == high_line + 1, low, 0.0))
    marks = lax.dot_general(
        marks.astype(jnp.bfloat16),
        as_bf16(iota((LANES, docs), 0) == position),
        NT,
        preferred_element_type=jnp.float32,
    )
    rows_copy.wait()
    rows = rows_ref[...]
    squares = jnp.sum(rows * rows, axis=1, keepdims=True)
    unit = (rows * lax.rsqrt(squares + epsilon)).astype(jnp.bfloat16)
    line = iota((GROUPS, SLOTS, LANES), 1).astype(jnp.float32).astype(jnp.bfloat16)
    carried = None
    for at in range(CHUNKS):
        part = slice(at * PART, (at + 1) * PART)
        packed = jnp.dot(place[part], unit, preferred_element_type=jnp.float32)
        packed = packed.astype(jnp.bfloat16)
        mine = line >= jnp.asarray(at * 2, jnp.bfloat16)
        for lane in range(0, width, LANES):
            tile = packed[:, lane : lane + LANES].reshape(GROUPS, SLOTS, LANES)
            value = tile if carried is None else jnp.where(mine, tile, carried)
            out_ref[:, at * 8 + lane // LANES] = value
            carried = tile
        mark = marks[part].astype(jnp.bfloat16).reshape(GROUPS, SLOTS, LANES)
        carried = jnp.where(mine, mark, carried)
    out_ref[:, TILES - 1] = carried


def unfold(ref):
    slot = iota((GROUPS, SLOTS, LANES), 1)
    lane = iota((GROUPS, SLOTS, LANES), 2)
    rows, ranks = [], []
    for chunk in range(CHUNKS):
        turn = chunk * 2
        tiles = [ref[:, chunk * 8 + i] for i in range(9)]
        if chunk > 0:
            line = slot.astype(jnp.float32).astype(jnp.bfloat16)
            mine = line >= jnp.asarray(turn, jnp.bfloat16)
            data = [jnp.where(mine, x, y) for x, y in zip(tiles[:-1], tiles[1:])]
        else:
            data = tiles[:-1]
        rows.append(jnp.concatenate([x.reshape(PART, LANES) for x in data], axis=1))
        marks = tiles[-1].astype(jnp.float32)
        rank = marks[:, turn : turn + 1] * 16.0 + marks[:, turn + 1 : turn + 2]
        mine = lane == (slot - turn) % SLOTS
        rank = jnp.sum(jnp.where(mine, rank, 0.0), axis=2, keepdims=True)
        ranks.append(jnp.broadcast_to(rank, (GROUPS, SLOTS, LANES)).reshape(PART, LANES))
    return jnp.concatenate(rows, axis=0), jnp.concatenate(ranks, axis=0)


def largest(values):
    return jnp.max(values.reshape(-1, 8, values.shape[1]), axis=0)


def similarities(keys, queries_ref):
    step = 2 * LANES
    for at in range(0, queries_ref.shape[1], step):
        similar = jnp.dot(
            keys, queries_ref[: keys.shape[1], at : at + step], preferred_element_type=jnp.float32
        )
        for lane in range(0, step, LANES):
            yield at + lane, similar[:, lane : lane + LANES]


def maxima(keys, key_rank, queries_ref, query_rank):
    for at, similar in similarities(keys, queries_ref):
        allowed = key_rank < query_rank[0:1, at : at + LANES]
        yield at, largest(jnp.where(allowed, similar, -1.0))


def turn_kernel(early_ref, turned_ref, best_ref):
    core = lax.axis_index("core")
    width = turned_ref.shape[0] - MARKS

    @pl.when(core == 0)
    def _():
        best_ref[...] = jnp.full(best_ref.shape, -1.0, jnp.float32)

    @pl.when(core != 0)
    def _():
        rows, ranks = unfold(early_ref)
        turned_ref[:width] = rows.T
        rank = ranks.T[0:MARKS]
        high = jnp.floor(rank * 0.0625)
        parts = jnp.where(iota(rank.shape, 0) == 0, high, rank - high * 16.0)
        turned_ref[width:] = parts.astype(jnp.bfloat16)
        for at, best in maxima(rows, ranks, turned_ref, rank):
            best_ref[:, at : at + LANES] = best


def first_kernel(late_ref, other_ref, cross_ref, away_ref):
    core = lax.axis_index("core")
    width = other_ref.shape[0] - MARKS

    @pl.when(core == 0)
    def _():
        rows, ranks = unfold(late_ref)
        marks = other_ref[width:].astype(jnp.float32)
        other_rank = marks[0:1] * 16.0 + marks[1:2]
        best = jnp.full(ranks.shape, -1.0, jnp.float32)
        for at, similar in similarities(rows, other_ref):
            rank = other_rank[:, at : at + LANES]
            away_ref[:, at : at + LANES] = largest(jnp.where(ranks < rank, similar, -1.0))
            best = jnp.maximum(best, jnp.where(rank < ranks, similar, -1.0))
        cross_ref[...] = best

    @pl.when(core != 0)
    def _():
        away_ref[...] = jnp.full(away_ref.shape, -1.0, jnp.float32)
        cross_ref[...] = jnp.full(cross_ref.shape, -1.0, jnp.float32)


def lines_of(best_ref, best):
    best = jnp.max(best, axis=0, keepdims=True)
    lines = [best[:, at : at + LANES] for at in range(0, best.shape[1], LANES)]
    lines = jnp.concatenate(lines + lines)
    for at in range(0, CLUSTERS, 8):
        best_ref[at : at + 8] = lines


def second_kernel(late_ref, cross_ref, out_ref, queries_ref):
    @pl.when(lax.axis_index("core") == 0)
    def _():
        rows, ranks = unfold(late_ref)
        queries_ref[...] = rows.T
        cross = largest(cross_ref[...].T)
        best = [x for _, x in maxima(rows, ranks, queries_ref, ranks.T[0:8])]
        lines_of(out_ref, jnp.maximum(jnp.concatenate(best, axis=1), cross))


def merge_kernel(first_ref, away_ref, out_ref):
    @pl.when(lax.axis_index("core") != 0)
    def _():
        lines_of(out_ref, jnp.maximum(first_ref[...], away_ref[...]))


def unpack_kernel(best_ref, where_ref, out_ref):
    docs = where_ref.shape[1]
    best = jnp.concatenate([best_ref[...], jnp.zeros((LANES - CLUSTERS, LANES), jnp.float32)])
    cluster = jnp.broadcast_to(where_ref[0:1], (LANES, docs))
    by_cluster = jnp.take_along_axis(best.T, cluster, axis=1)
    wanted = iota((LANES, docs), 0) == where_ref[1:2]
    out_ref[...] = jnp.sum(jnp.where(wanted, by_cluster, 0.0), axis=0, keepdims=True)


def call(kernel, out_shape, flops, moved, **more):
    return pl.pallas_call(
        kernel,
        out_shape=out_shape,
        compiler_params=pltpu.CompilerParams(vmem_limit_bytes=VMEM),
        cost_estimate=pl.CostEstimate(flops=flops, bytes_accessed=moved, transcendentals=0),
        **more,
    )


def in_hbm(x):
    return pltpu.with_memory_space_constraint(x, pltpu.HBM)


def per_device(embeddings, cluster, order):
    docs, width = embeddings.shape
    slots = CLUSTERS * SLOTS
    shape = jax.ShapeDtypeStruct
    f32, bf16, i32 = jnp.float32, jnp.bfloat16, jnp.int32
    tiles = (GROUPS, TILES, 8, LANES)
    moved = CLUSTERS * (SLOTS * width + 2 * LANES) * 2
    packed, where = call(
        pack_kernel,
        (shape(tiles, bf16), shape((8, docs), i32)),
        2 * slots * docs * width,
        docs * width * 4 + moved,
        in_specs=[pl.BlockSpec(memory_space=pltpu.HBM)] * 3,
        scratch_shapes=[
            pltpu.VMEM((docs, width), f32),
            pltpu.VMEM((2, 1, docs), i32),
            pltpu.SemaphoreType.DMA((3,)),
        ],
    )(*(in_hbm(x) for x in (embeddings, cluster.reshape(1, docs), order.reshape(1, docs))))
    chunks = packed.reshape(CLUSTERS, TILES, 2, LANES)

    def exchange(sent):
        return lax.all_to_all(sent, ("x", "zy"), split_axis=0, concat_axis=0, tiled=True)

    def keep(sent):
        return sent

    core = lax.axis_index("core")
    early = lax.cond(core == 1, exchange, keep, chunks)
    late = lax.cond(core == 0, exchange, keep, chunks).reshape(tiles)
    flops = 2 * slots * slots * width
    line = shape((8, slots), f32)
    turned, first = call(
        turn_kernel,
        (pltpu.VMEM((width + MARKS, slots), bf16), pltpu.VMEM((8, slots), f32)),
        flops,
        2 * moved,
    )(pltpu.with_memory_space_constraint(early.reshape(tiles), pltpu.VMEM))
    other = lax.ppermute(turned, "core", [(1, 0)])
    cross, away = call(first_kernel, (shape((slots, LANES), f32), line), flops, 2 * moved)(
        late, other
    )
    away = lax.ppermute(away, "core", [(0, 1), (1, 0)])
    answer = shape((CLUSTERS, LANES), f32)
    best = call(
        second_kernel,
        answer,
        flops,
        2 * moved,
        scratch_shapes=[pltpu.VMEM((width, slots), bf16)],
    )(late, cross)
    back = lax.cond(core == 0, exchange, keep, best)
    best = call(merge_kernel, answer, 0, CLUSTERS * LANES * 4)(first, away)
    back = lax.cond(core == 1, lambda sent, kept: exchange(sent), lambda sent, kept: kept, best, back)
    result = call(unpack_kernel, shape((1, docs), f32), 0, CLUSTERS * LANES * 4)(back, where)
    return result.reshape(docs)


def solution(mesh):
    devices = mesh.devices.reshape(-1, CORES, mesh.shape["narrow"])
    chips = Mesh(devices, ("zy", "core", "x"))
    axes = ("zy", "core", "x")
    return jax.shard_map(
        per_device,
        mesh=chips,
        in_specs=(P(axes, None), P(axes), P(axes)),
        out_specs=P(axes),
        check_vma=False,
    )
```

```python
import jax
import jax.numpy as jnp
from jax import lax
from jax.experimental import pallas as pl
from jax.experimental.pallas import tpu as pltpu
from jax.sharding import Mesh, PartitionSpec as P

CLUSTERS = 64
SLOTS = 8
CAP = 512
LANES = 128
CORES = 2
CHUNKS = 4
GROUPS = CLUSTERS // CHUNKS
PART = GROUPS * SLOTS
TILES = 33
MARKS = 16
epsilon = 1e-06

VMEM = 32 * 1024 * 1024
NT = (((1,), (1,)), ((), ()))


def iota(shape, axis):
    return lax.broadcasted_iota(jnp.int32, shape, axis)


def as_bf16(mask):
    return jnp.where(mask, 1.0, 0.0).astype(jnp.bfloat16)


def pack_kernel(rows_hbm, cluster_hbm, order_hbm, out_ref, where_ref, rows_ref, ids_ref, sems):
    docs, width = rows_ref.shape
    cluster_copy = pltpu.make_async_copy(cluster_hbm, ids_ref.at[0], sems.at[0])
    order_copy = pltpu.make_async_copy(order_hbm, ids_ref.at[1], sems.at[1])
    rows_copy = pltpu.make_async_copy(rows_hbm, rows_ref, sems.at[2])
    cluster_copy.start()
    order_copy.start()
    rows_copy.start()
    before = as_bf16(iota((docs, docs), 0) < iota((docs, docs), 1))
    cluster_copy.wait()
    order_copy.wait()
    cluster = ids_ref[0]
    member = iota((CLUSTERS, docs), 0) == cluster
    count = jnp.dot(as_bf16(member), before, preferred_element_type=jnp.float32)
    position = jnp.sum(jnp.where(member, count, 0.0), axis=0, keepdims=True).astype(jnp.int32)
    chip = lax.axis_index("x") * lax.axis_size("zy") + lax.axis_index("zy")
    where_ref[0:1] = cluster
    where_ref[1:2] = chip // CHUNKS * SLOTS + (chip % CHUNKS * 2 + position) % SLOTS
    chunk = cluster % CHUNKS
    start = chunk * PART + cluster // CHUNKS * SLOTS
    line = iota((CHUNKS * PART, docs), 0)
    place = as_bf16(line == start + (chunk * 2 + position) % SLOTS)
    rank = ids_ref[1] - CAP
    high = (rank >> 4).astype(jnp.float32)
    low = (rank & 15).astype(jnp.float32)
    high_line = start + chunk * 2
    marks = jnp.where(line == high_line, high, jnp.where(line == high_line + 1, low, 0.0))
    marks = lax.dot_general(
        marks.astype(jnp.bfloat16),
        as_bf16(iota((LANES, docs), 0) == position),
        NT,
        preferred_element_type=jnp.float32,
    )
    rows_copy.wait()
    rows = rows_ref[...]
    squares = jnp.sum(rows * rows, axis=1, keepdims=True)
    unit = (rows * lax.rsqrt(squares + epsilon)).astype(jnp.bfloat16)
    line = iota((GROUPS, SLOTS, LANES), 1).astype(jnp.float32).astype(jnp.bfloat16)
    carried = None
    for at in range(CHUNKS):
        part = slice(at * PART, (at + 1) * PART)
        packed = jnp.dot(place[part], unit, preferred_element_type=jnp.float32)
        packed = packed.astype(jnp.bfloat16)
        mine = line >= jnp.asarray(at * 2, jnp.bfloat16)
        for lane in range(0, width, LANES):
            tile = packed[:, lane : lane + LANES].reshape(GROUPS, SLOTS, LANES)
            value = tile if carried is None else jnp.where(mine, tile, carried)
            out_ref[:, at * 8 + lane // LANES] = value
            carried = tile
        mark = marks[part].astype(jnp.bfloat16).reshape(GROUPS, SLOTS, LANES)
        carried = jnp.where(mine, mark, carried)
    out_ref[:, TILES - 1] = carried


def unfold(ref):
    slot = iota((GROUPS, SLOTS, LANES), 1)
    lane = iota((GROUPS, SLOTS, LANES), 2)
    rows, ranks = [], []
    for chunk in range(CHUNKS):
        turn = chunk * 2
        tiles = [ref[:, chunk * 8 + i] for i in range(9)]
        if chunk > 0:
            line = slot.astype(jnp.float32).astype(jnp.bfloat16)
            mine = line >= jnp.asarray(turn, jnp.bfloat16)
            data = [jnp.where(mine, x, y) for x, y in zip(tiles[:-1], tiles[1:])]
        else:
            data = tiles[:-1]
        rows.append(jnp.concatenate([x.reshape(PART, LANES) for x in data], axis=1))
        marks = tiles[-1].astype(jnp.float32)
        rank = marks[:, turn : turn + 1] * 16.0 + marks[:, turn + 1 : turn + 2]
        mine = lane == (slot - turn) % SLOTS
        rank = jnp.sum(jnp.where(mine, rank, 0.0), axis=2, keepdims=True)
        ranks.append(jnp.broadcast_to(rank, (GROUPS, SLOTS, LANES)).reshape(PART, LANES))
    return jnp.concatenate(rows, axis=0), jnp.concatenate(ranks, axis=0)


def largest(values):
    return jnp.max(values.reshape(-1, 8, values.shape[1]), axis=0)


def similarities(keys, queries_ref):
    step = 2 * LANES
    for at in range(0, queries_ref.shape[1], step):
        similar = jnp.dot(
            keys, queries_ref[: keys.shape[1], at : at + step], preferred_element_type=jnp.float32
        )
        for lane in range(0, step, LANES):
            yield at + lane, similar[:, lane : lane + LANES]


def maxima(keys, key_rank, queries_ref, query_rank):
    for at, similar in similarities(keys, queries_ref):
        allowed = key_rank < query_rank[0:1, at : at + LANES]
        yield at, largest(jnp.where(allowed, similar, -1.0))


def turn_kernel(early_ref, turned_ref, best_ref):
    core = lax.axis_index("core")
    width = turned_ref.shape[0] - MARKS

    @pl.when(core == 0)
    def _():
        best_ref[...] = jnp.full(best_ref.shape, -1.0, jnp.float32)

    @pl.when(core != 0)
    def _():
        rows, ranks = unfold(early_ref)
        turned_ref[:width] = rows.T
        rank = ranks.T[0:MARKS]
        high = jnp.floor(rank * 0.0625)
        parts = jnp.where(iota(rank.shape, 0) == 0, high, rank - high * 16.0)
        turned_ref[width:] = parts.astype(jnp.bfloat16)
        for at, best in maxima(rows, ranks, turned_ref, rank):
            best_ref[:, at : at + LANES] = best


def first_kernel(late_ref, other_ref, cross_ref, away_ref):
    core = lax.axis_index("core")
    width = other_ref.shape[0] - MARKS

    @pl.when(core == 0)
    def _():
        rows, ranks = unfold(late_ref)
        marks = other_ref[width:].astype(jnp.float32)
        other_rank = marks[0:1] * 16.0 + marks[1:2]
        best = jnp.full(ranks.shape, -1.0, jnp.float32)
        for at, similar in similarities(rows, other_ref):
            rank = other_rank[:, at : at + LANES]
            away_ref[:, at : at + LANES] = largest(jnp.where(ranks < rank, similar, -1.0))
            best = jnp.maximum(best, jnp.where(rank < ranks, similar, -1.0))
        cross_ref[...] = best

    @pl.when(core != 0)
    def _():
        away_ref[...] = jnp.full(away_ref.shape, -1.0, jnp.float32)
        cross_ref[...] = jnp.full(cross_ref.shape, -1.0, jnp.float32)


def lines_of(best_ref, best):
    best = jnp.max(best, axis=0, keepdims=True)
    lines = [best[:, at : at + LANES] for at in range(0, best.shape[1], LANES)]
    lines = jnp.concatenate(lines + lines)
    for at in range(0, CLUSTERS, 8):
        best_ref[at : at + 8] = lines


def second_kernel(late_ref, cross_ref, out_ref):
    @pl.when(lax.axis_index("core") == 0)
    def _():
        rows, ranks = unfold(late_ref)
        cross = largest(cross_ref[...].T)
        line = ranks.T[0:1]
        best = []
        step = 2 * LANES
        for at in range(0, rows.shape[0], step):
            similar = lax.dot_general(
                rows, rows[at : at + step], NT, preferred_element_type=jnp.float32
            )
            for lane in range(0, step, LANES):
                allowed = ranks < line[:, at + lane : at + lane + LANES]
                best.append(largest(jnp.where(allowed, similar[:, lane : lane + LANES], -1.0)))
        lines_of(out_ref, jnp.maximum(jnp.concatenate(best, axis=1), cross))


def merge_kernel(first_ref, away_ref, out_ref):
    @pl.when(lax.axis_index("core") != 0)
    def _():
        lines_of(out_ref, jnp.maximum(first_ref[...], away_ref[...]))


def unpack_kernel(best_ref, where_ref, out_ref):
    docs = where_ref.shape[1]
    best = jnp.concatenate([best_ref[...], jnp.zeros((LANES - CLUSTERS, LANES), jnp.float32)])
    cluster = jnp.broadcast_to(where_ref[0:1], (LANES, docs))
    by_cluster = jnp.take_along_axis(best.T, cluster, axis=1)
    wanted = iota((LANES, docs), 0) == where_ref[1:2]
    out_ref[...] = jnp.sum(jnp.where(wanted, by_cluster, 0.0), axis=0, keepdims=True)


def call(kernel, out_shape, flops, moved, **more):
    return pl.pallas_call(
        kernel,
        out_shape=out_shape,
        compiler_params=pltpu.CompilerParams(vmem_limit_bytes=VMEM),
        cost_estimate=pl.CostEstimate(flops=flops, bytes_accessed=moved, transcendentals=0),
        **more,
    )


def in_hbm(x):
    return pltpu.with_memory_space_constraint(x, pltpu.HBM)


def per_device(embeddings, cluster, order):
    docs, width = embeddings.shape
    slots = CLUSTERS * SLOTS
    shape = jax.ShapeDtypeStruct
    f32, bf16, i32 = jnp.float32, jnp.bfloat16, jnp.int32
    tiles = (GROUPS, TILES, 8, LANES)
    moved = CLUSTERS * (SLOTS * width + 2 * LANES) * 2
    packed, where = call(
        pack_kernel,
        (shape(tiles, bf16), shape((8, docs), i32)),
        2 * slots * docs * width,
        docs * width * 4 + moved,
        in_specs=[pl.BlockSpec(memory_space=pltpu.HBM)] * 3,
        scratch_shapes=[
            pltpu.VMEM((docs, width), f32),
            pltpu.VMEM((2, 1, docs), i32),
            pltpu.SemaphoreType.DMA((3,)),
        ],
    )(*(in_hbm(x) for x in (embeddings, cluster.reshape(1, docs), order.reshape(1, docs))))
    chunks = packed.reshape(CLUSTERS, TILES, 2, LANES)

    def exchange(sent):
        return lax.all_to_all(sent, ("x", "zy"), split_axis=0, concat_axis=0, tiled=True)

    def keep(sent):
        return sent

    core = lax.axis_index("core")
    early = lax.cond(core == 1, exchange, keep, chunks)
    late = lax.cond(core == 0, exchange, keep, chunks).reshape(tiles)
    flops = 2 * slots * slots * width
    line = shape((8, slots), f32)
    turned, first = call(
        turn_kernel,
        (pltpu.VMEM((width + MARKS, slots), bf16), pltpu.VMEM((8, slots), f32)),
        flops,
        2 * moved,
    )(pltpu.with_memory_space_constraint(early.reshape(tiles), pltpu.VMEM))
    other = lax.ppermute(turned, "core", [(1, 0)])
    cross, away = call(first_kernel, (shape((slots, LANES), f32), line), flops, 2 * moved)(
        late, other
    )
    away = lax.ppermute(away, "core", [(0, 1), (1, 0)])
    answer = shape((CLUSTERS, LANES), f32)
    best = call(
        second_kernel,
        answer,
        flops,
        2 * moved,
    )(late, cross)
    back = lax.cond(core == 0, exchange, keep, best)
    best = call(merge_kernel, answer, 0, CLUSTERS * LANES * 4)(first, away)
    back = lax.cond(core == 1, lambda sent, kept: exchange(sent), lambda sent, kept: kept, best, back)
    result = call(unpack_kernel, shape((1, docs), f32), 0, CLUSTERS * LANES * 4)(back, where)
    return result.reshape(docs)


def solution(mesh):
    devices = mesh.devices.reshape(-1, CORES, mesh.shape["narrow"])
    chips = Mesh(devices, ("zy", "core", "x"))
    axes = ("zy", "core", "x")
    return jax.shard_map(
        per_device,
        mesh=chips,
        in_specs=(P(axes, None), P(axes), P(axes)),
        out_specs=P(axes),
        check_vma=False,
    )
```

```python
import jax
import jax.numpy as jnp
from jax import lax
from jax.experimental import pallas as pl
from jax.experimental.pallas import tpu as pltpu
from jax.sharding import Mesh, PartitionSpec as P

CLUSTERS = 64
SLOTS = 8
CAP = 512
LANES = 128
CORES = 2
CHUNKS = 4
GROUPS = CLUSTERS // CHUNKS
PART = GROUPS * SLOTS
TILES = 33
MARKS = 16
epsilon = 1e-06

VMEM = 32 * 1024 * 1024
NT = (((1,), (1,)), ((), ()))
TN = (((0,), (0,)), ((), ()))


def iota(shape, axis):
    return lax.broadcasted_iota(jnp.int32, shape, axis)


def as_bf16(mask):
    return jnp.where(mask, 1.0, 0.0).astype(jnp.bfloat16)


def pack_kernel(rows_hbm, cluster_hbm, order_hbm, out_ref, where_ref, rows_ref, ids_ref, sems):
    docs, width = rows_ref.shape
    cluster_copy = pltpu.make_async_copy(cluster_hbm, ids_ref.at[0], sems.at[0])
    order_copy = pltpu.make_async_copy(order_hbm, ids_ref.at[1], sems.at[1])
    rows_copy = pltpu.make_async_copy(rows_hbm, rows_ref, sems.at[2])
    cluster_copy.start()
    order_copy.start()
    rows_copy.start()
    before = as_bf16(iota((docs, docs), 0) < iota((docs, docs), 1))
    cluster_copy.wait()
    order_copy.wait()
    cluster = ids_ref[0]
    member = iota((CLUSTERS, docs), 0) == cluster
    count = jnp.dot(as_bf16(member), before, preferred_element_type=jnp.float32)
    position = jnp.sum(jnp.where(member, count, 0.0), axis=0, keepdims=True).astype(jnp.int32)
    chip = lax.axis_index("x") * lax.axis_size("zy") + lax.axis_index("zy")
    where_ref[0:1] = cluster
    where_ref[1:2] = chip // CHUNKS * SLOTS + (chip % CHUNKS * 2 + position) % SLOTS
    chunk = cluster % CHUNKS
    start = chunk * PART + cluster // CHUNKS * SLOTS
    line = iota((CHUNKS * PART, docs), 0)
    place = as_bf16(line == start + (chunk * 2 + position) % SLOTS)
    rank = ids_ref[1] - CAP
    high = (rank >> 4).astype(jnp.float32)
    low = (rank & 15).astype(jnp.float32)
    high_line = start + chunk * 2
    marks = jnp.where(line == high_line, high, jnp.where(line == high_line + 1, low, 0.0))
    marks = lax.dot_general(
        marks.astype(jnp.bfloat16),
        as_bf16(iota((LANES, docs), 0) == position),
        NT,
        preferred_element_type=jnp.float32,
    )
    rows_copy.wait()
    rows = rows_ref[...]
    squares = jnp.sum(rows * rows, axis=1, keepdims=True)
    unit = (rows * lax.rsqrt(squares + epsilon)).astype(jnp.bfloat16)
    line = iota((GROUPS, SLOTS, LANES), 1).astype(jnp.float32).astype(jnp.bfloat16)
    carried = None
    for at in range(CHUNKS):
        part = slice(at * PART, (at + 1) * PART)
        packed = jnp.dot(place[part], unit, preferred_element_type=jnp.float32)
        packed = packed.astype(jnp.bfloat16)
        mine = line >= jnp.asarray(at * 2, jnp.bfloat16)
        for lane in range(0, width, LANES):
            tile = packed[:, lane : lane + LANES].reshape(GROUPS, SLOTS, LANES)
            value = tile if carried is None else jnp.where(mine, tile, carried)
            out_ref[:, at * 8 + lane // LANES] = value
            carried = tile
        mark = marks[part].astype(jnp.bfloat16).reshape(GROUPS, SLOTS, LANES)
        carried = jnp.where(mine, mark, carried)
    out_ref[:, TILES - 1] = carried


def unfold(ref):
    slot = iota((GROUPS, SLOTS, LANES), 1)
    lane = iota((GROUPS, SLOTS, LANES), 2)
    rows, ranks = [], []
    for chunk in range(CHUNKS):
        turn = chunk * 2
        tiles = [ref[:, chunk * 8 + i] for i in range(9)]
        if chunk > 0:
            line = slot.astype(jnp.float32).astype(jnp.bfloat16)
            mine = line >= jnp.asarray(turn, jnp.bfloat16)
            data = [jnp.where(mine, x, y) for x, y in zip(tiles[:-1], tiles[1:])]
        else:
            data = tiles[:-1]
        rows.append(jnp.concatenate([x.reshape(PART, LANES) for x in data], axis=1))
        marks = tiles[-1].astype(jnp.float32)
        rank = marks[:, turn : turn + 1] * 16.0 + marks[:, turn + 1 : turn + 2]
        mine = lane == (slot - turn) % SLOTS
        rank = jnp.sum(jnp.where(mine, rank, 0.0), axis=2, keepdims=True)
        ranks.append(jnp.broadcast_to(rank, (GROUPS, SLOTS, LANES)).reshape(PART, LANES))
    return jnp.concatenate(rows, axis=0), jnp.concatenate(ranks, axis=0)


def largest(values):
    return jnp.max(values.reshape(-1, 8, values.shape[1]), axis=0)


def similarities(keys, queries_ref):
    step = 2 * LANES
    for at in range(0, queries_ref.shape[1], step):
        similar = jnp.dot(
            keys, queries_ref[: keys.shape[1], at : at + step], preferred_element_type=jnp.float32
        )
        for lane in range(0, step, LANES):
            yield at + lane, similar[:, lane : lane + LANES]


def maxima(keys, key_rank, queries_ref, query_rank):
    for at, similar in similarities(keys, queries_ref):
        allowed = key_rank < query_rank[0:1, at : at + LANES]
        yield at, largest(jnp.where(allowed, similar, -1.0))


def turn_kernel(early_ref, turned_ref):
    width = turned_ref.shape[0] - MARKS

    @pl.when(lax.axis_index("core") != 0)
    def _():
        rows, ranks = unfold(early_ref)
        turned_ref[:width] = rows.T
        rank = ranks.T[0:MARKS]
        high = jnp.floor(rank * 0.0625)
        parts = jnp.where(iota(rank.shape, 0) == 0, high, rank - high * 16.0)
        turned_ref[width:] = parts.astype(jnp.bfloat16)


def first_kernel(late_ref, other_ref, cross_ref, away_ref):
    core = lax.axis_index("core")
    width = other_ref.shape[0] - MARKS

    @pl.when(core == 0)
    def _():
        rows, ranks = unfold(late_ref)
        marks = other_ref[width:].astype(jnp.float32)
        other_rank = marks[0:1] * 16.0 + marks[1:2]
        best = jnp.full(ranks.shape, -1.0, jnp.float32)
        for at, similar in similarities(rows, other_ref):
            rank = other_rank[:, at : at + LANES]
            away_ref[:, at : at + LANES] = largest(jnp.where(ranks < rank, similar, -1.0))
            best = jnp.maximum(best, jnp.where(rank < ranks, similar, -1.0))
        cross_ref[...] = best

    @pl.when(core != 0)
    def _():
        away_ref[...] = jnp.full(away_ref.shape, -1.0, jnp.float32)
        cross_ref[...] = jnp.full(cross_ref.shape, -1.0, jnp.float32)


def lines_of(best_ref, best):
    best = jnp.max(best, axis=0, keepdims=True)
    lines = [best[:, at : at + LANES] for at in range(0, best.shape[1], LANES)]
    lines = jnp.concatenate(lines + lines)
    for at in range(0, CLUSTERS, 8):
        best_ref[at : at + 8] = lines


def second_kernel(late_ref, cross_ref, mine_ref, out_ref, first_ref):
    @pl.when(lax.axis_index("core") == 0)
    def _():
        rows, ranks = unfold(late_ref)
        cross = largest(cross_ref[...].T)
        line = ranks.T[0:1]
        best = []
        step = 2 * LANES
        for at in range(0, rows.shape[0], step):
            similar = lax.dot_general(
                rows, rows[at : at + step], NT, preferred_element_type=jnp.float32
            )
            for lane in range(0, step, LANES):
                allowed = ranks < line[:, at + lane : at + lane + LANES]
                best.append(largest(jnp.where(allowed, similar[:, lane : lane + LANES], -1.0)))
        lines_of(out_ref, jnp.maximum(jnp.concatenate(best, axis=1), cross))

    @pl.when(lax.axis_index("core") != 0)
    def _():
        width = mine_ref.shape[0] - MARKS
        marks = mine_ref[width:].astype(jnp.float32)
        line = marks[0:1] * 16.0 + marks[1:2]
        ranks = jnp.broadcast_to(line, (LANES, line.shape[1])).T
        step = 2 * LANES
        for at in range(0, line.shape[1], step):
            similar = lax.dot_general(
                mine_ref[:width],
                mine_ref[:width, at : at + step],
                TN,
                preferred_element_type=jnp.float32,
            )
            for lane in range(0, step, LANES):
                allowed = ranks < line[:, at + lane : at + lane + LANES]
                best = largest(jnp.where(allowed, similar[:, lane : lane + LANES], -1.0))
                first_ref[:, at + lane : at + lane + LANES] = best


def merge_kernel(first_ref, away_ref, out_ref):
    @pl.when(lax.axis_index("core") != 0)
    def _():
        lines_of(out_ref, jnp.maximum(first_ref[...], away_ref[...]))


def unpack_kernel(best_ref, where_ref, out_ref):
    docs = where_ref.shape[1]
    best = jnp.concatenate([best_ref[...], jnp.zeros((LANES - CLUSTERS, LANES), jnp.float32)])
    cluster = jnp.broadcast_to(where_ref[0:1], (LANES, docs))
    by_cluster = jnp.take_along_axis(best.T, cluster, axis=1)
    wanted = iota((LANES, docs), 0) == where_ref[1:2]
    out_ref[...] = jnp.sum(jnp.where(wanted, by_cluster, 0.0), axis=0, keepdims=True)


def call(kernel, out_shape, flops, moved, **more):
    return pl.pallas_call(
        kernel,
        out_shape=out_shape,
        compiler_params=pltpu.CompilerParams(vmem_limit_bytes=VMEM),
        cost_estimate=pl.CostEstimate(flops=flops, bytes_accessed=moved, transcendentals=0),
        **more,
    )


def in_hbm(x):
    return pltpu.with_memory_space_constraint(x, pltpu.HBM)


def per_device(embeddings, cluster, order):
    docs, width = embeddings.shape
    slots = CLUSTERS * SLOTS
    shape = jax.ShapeDtypeStruct
    f32, bf16, i32 = jnp.float32, jnp.bfloat16, jnp.int32
    tiles = (GROUPS, TILES, 8, LANES)
    moved = CLUSTERS * (SLOTS * width + 2 * LANES) * 2
    packed, where = call(
        pack_kernel,
        (shape(tiles, bf16), shape((8, docs), i32)),
        2 * slots * docs * width,
        docs * width * 4 + moved,
        in_specs=[pl.BlockSpec(memory_space=pltpu.HBM)] * 3,
        scratch_shapes=[
            pltpu.VMEM((docs, width), f32),
            pltpu.VMEM((2, 1, docs), i32),
            pltpu.SemaphoreType.DMA((3,)),
        ],
    )(*(in_hbm(x) for x in (embeddings, cluster.reshape(1, docs), order.reshape(1, docs))))
    chunks = packed.reshape(CLUSTERS, TILES, 2, LANES)

    def exchange(sent):
        return lax.all_to_all(sent, ("x", "zy"), split_axis=0, concat_axis=0, tiled=True)

    def keep(sent):
        return sent

    core = lax.axis_index("core")
    early = lax.cond(core == 1, exchange, keep, chunks)
    late = lax.cond(core == 0, exchange, keep, chunks).reshape(tiles)
    flops = 2 * slots * slots * width
    line = shape((8, slots), f32)
    turned = call(turn_kernel, pltpu.VMEM((width + MARKS, slots), bf16), 0, 2 * moved)(
        pltpu.with_memory_space_constraint(early.reshape(tiles), pltpu.VMEM)
    )
    other = lax.ppermute(turned, "core", [(1, 0)])
    cross, away = call(first_kernel, (shape((slots, LANES), f32), line), flops, 2 * moved)(
        late, other
    )
    away = lax.ppermute(away, "core", [(0, 1), (1, 0)])
    answer = shape((CLUSTERS, LANES), f32)
    mine = pltpu.with_memory_space_constraint(turned, pltpu.VMEM)
    best, first = call(second_kernel, (answer, line), flops, 2 * moved)(late, cross, mine)
    back = lax.cond(core == 0, exchange, keep, best)
    best = call(merge_kernel, answer, 0, CLUSTERS * LANES * 4)(first, away)
    back = lax.cond(core == 1, lambda sent, kept: exchange(sent), lambda sent, kept: kept, best, back)
    result = call(unpack_kernel, shape((1, docs), f32), 0, CLUSTERS * LANES * 4)(back, where)
    return result.reshape(docs)


def solution(mesh):
    devices = mesh.devices.reshape(-1, CORES, mesh.shape["narrow"])
    chips = Mesh(devices, ("zy", "core", "x"))
    axes = ("zy", "core", "x")
    return jax.shard_map(
        per_device,
        mesh=chips,
        in_specs=(P(axes, None), P(axes), P(axes)),
        out_specs=P(axes),
        check_vma=False,
    )
```

```python
import jax
import jax.numpy as jnp
from jax import lax
from jax.experimental import pallas as pl
from jax.experimental.pallas import tpu as pltpu
from jax.sharding import Mesh, PartitionSpec as P

CLUSTERS = 64
SLOTS = 8
CAP = 512
LANES = 128
CORES = 2
CHUNKS = 4
GROUPS = CLUSTERS // CHUNKS
PART = GROUPS * SLOTS
TILES = 33
MARKS = 16
epsilon = 1e-06

VMEM = 32 * 1024 * 1024
NT = (((1,), (1,)), ((), ()))
TN = (((0,), (0,)), ((), ()))


def iota(shape, axis):
    return lax.broadcasted_iota(jnp.int32, shape, axis)


def as_bf16(mask):
    return jnp.where(mask, 1.0, 0.0).astype(jnp.bfloat16)


def pack_kernel(rows_hbm, cluster_hbm, order_hbm, out_ref, where_ref, rows_ref, ids_ref, sems):
    docs, width = rows_ref.shape
    cluster_copy = pltpu.make_async_copy(cluster_hbm, ids_ref.at[0], sems.at[0])
    order_copy = pltpu.make_async_copy(order_hbm, ids_ref.at[1], sems.at[1])
    rows_copy = pltpu.make_async_copy(rows_hbm, rows_ref, sems.at[2])
    cluster_copy.start()
    order_copy.start()
    rows_copy.start()
    before = as_bf16(iota((docs, docs), 0) < iota((docs, docs), 1))
    cluster_copy.wait()
    order_copy.wait()
    cluster = ids_ref[0]
    member = iota((CLUSTERS, docs), 0) == cluster
    count = jnp.dot(as_bf16(member), before, preferred_element_type=jnp.float32)
    position = jnp.sum(jnp.where(member, count, 0.0), axis=0, keepdims=True).astype(jnp.int32)
    chip = lax.axis_index("x") * lax.axis_size("zy") + lax.axis_index("zy")
    where_ref[0:1] = cluster
    where_ref[1:2] = chip // CHUNKS * SLOTS + (chip % CHUNKS * 2 + position) % SLOTS
    chunk = cluster % CHUNKS
    start = chunk * PART + cluster // CHUNKS * SLOTS
    line = iota((CHUNKS * PART, docs), 0)
    place = as_bf16(line == start + (chunk * 2 + position) % SLOTS)
    rank = ids_ref[1] - CAP
    high = (rank >> 4).astype(jnp.float32)
    low = (rank & 15).astype(jnp.float32)
    high_line = start + chunk * 2
    marks = jnp.where(line == high_line, high, jnp.where(line == high_line + 1, low, 0.0))
    marks = lax.dot_general(
        marks.astype(jnp.bfloat16),
        as_bf16(iota((LANES, docs), 0) == position),
        NT,
        preferred_element_type=jnp.float32,
    )
    rows_copy.wait()
    rows = rows_ref[...]
    squares = jnp.sum(rows * rows, axis=1, keepdims=True)
    unit = (rows * lax.rsqrt(squares + epsilon)).astype(jnp.bfloat16)
    line = iota((GROUPS, SLOTS, LANES), 1).astype(jnp.float32).astype(jnp.bfloat16)
    carried = None
    for at in range(CHUNKS):
        part = slice(at * PART, (at + 1) * PART)
        packed = jnp.dot(place[part], unit, preferred_element_type=jnp.float32)
        packed = packed.astype(jnp.bfloat16)
        mine = line >= jnp.asarray(at * 2, jnp.bfloat16)
        for lane in range(0, width, LANES):
            tile = packed[:, lane : lane + LANES].reshape(GROUPS, SLOTS, LANES)
            value = tile if carried is None else jnp.where(mine, tile, carried)
            out_ref[:, at * 8 + lane // LANES] = value
            carried = tile
        mark = marks[part].astype(jnp.bfloat16).reshape(GROUPS, SLOTS, LANES)
        carried = jnp.where(mine, mark, carried)
    out_ref[:, TILES - 1] = carried


def unfold(ref):
    slot = iota((GROUPS, SLOTS, LANES), 1)
    lane = iota((GROUPS, SLOTS, LANES), 2)
    rows, ranks = [], []
    for chunk in range(CHUNKS):
        turn = chunk * 2
        tiles = [ref[:, chunk * 8 + i] for i in range(9)]
        if chunk > 0:
            line = slot.astype(jnp.float32).astype(jnp.bfloat16)
            mine = line >= jnp.asarray(turn, jnp.bfloat16)
            data = [jnp.where(mine, x, y) for x, y in zip(tiles[:-1], tiles[1:])]
        else:
            data = tiles[:-1]
        rows.append(jnp.concatenate([x.reshape(PART, LANES) for x in data], axis=1))
        marks = tiles[-1].astype(jnp.float32)
        rank = marks[:, turn : turn + 1] * 16.0 + marks[:, turn + 1 : turn + 2]
        mine = lane == (slot - turn) % SLOTS
        rank = jnp.sum(jnp.where(mine, rank, 0.0), axis=2, keepdims=True)
        ranks.append(jnp.broadcast_to(rank, (GROUPS, SLOTS, LANES)).reshape(PART, LANES))
    return jnp.concatenate(rows, axis=0), jnp.concatenate(ranks, axis=0)


def largest(values):
    return jnp.max(values.reshape(-1, 8, values.shape[1]), axis=0)


def similarities(keys, queries_ref):
    step = 4 * LANES
    for at in range(0, queries_ref.shape[1], step):
        similar = jnp.dot(
            keys, queries_ref[: keys.shape[1], at : at + step], preferred_element_type=jnp.float32
        )
        for lane in range(0, step, LANES):
            yield at + lane, similar[:, lane : lane + LANES]


def maxima(keys, key_rank, queries_ref, query_rank):
    for at, similar in similarities(keys, queries_ref):
        allowed = key_rank < query_rank[0:1, at : at + LANES]
        yield at, largest(jnp.where(allowed, similar, -1.0))


def turn_kernel(early_ref, turned_ref):
    width = turned_ref.shape[0] - MARKS

    @pl.when(lax.axis_index("core") != 0)
    def _():
        rows, ranks = unfold(early_ref)
        turned_ref[:width] = rows.T
        rank = ranks.T[0:MARKS]
        high = jnp.floor(rank * 0.0625)
        parts = jnp.where(iota(rank.shape, 0) == 0, high, rank - high * 16.0)
        turned_ref[width:] = parts.astype(jnp.bfloat16)


def first_kernel(late_ref, other_ref, cross_ref, away_ref):
    core = lax.axis_index("core")
    width = other_ref.shape[0] - MARKS

    @pl.when(core == 0)
    def _():
        rows, ranks = unfold(late_ref)
        marks = other_ref[width:].astype(jnp.float32)
        other_rank = marks[0:1] * 16.0 + marks[1:2]
        best = jnp.full(ranks.shape, -1.0, jnp.float32)
        for at, similar in similarities(rows, other_ref):
            rank = other_rank[:, at : at + LANES]
            away_ref[:, at : at + LANES] = largest(jnp.where(ranks < rank, similar, -1.0))
            best = jnp.maximum(best, jnp.where(rank < ranks, similar, -1.0))
        cross_ref[...] = best

    @pl.when(core != 0)
    def _():
        away_ref[...] = jnp.full(away_ref.shape, -1.0, jnp.float32)
        cross_ref[...] = jnp.full(cross_ref.shape, -1.0, jnp.float32)


def lines_of(best_ref, best):
    best = jnp.max(best, axis=0, keepdims=True)
    lines = [best[:, at : at + LANES] for at in range(0, best.shape[1], LANES)]
    lines = jnp.concatenate(lines + lines)
    for at in range(0, CLUSTERS, 8):
        best_ref[at : at + 8] = lines


def second_kernel(late_ref, cross_ref, mine_ref, out_ref, first_ref):
    @pl.when(lax.axis_index("core") == 0)
    def _():
        rows, ranks = unfold(late_ref)
        cross = largest(cross_ref[...].T)
        line = ranks.T[0:1]
        best = []
        step = 4 * LANES
        for at in range(0, rows.shape[0], step):
            similar = lax.dot_general(
                rows, rows[at : at + step], NT, preferred_element_type=jnp.float32
            )
            for lane in range(0, step, LANES):
                allowed = ranks < line[:, at + lane : at + lane + LANES]
                best.append(largest(jnp.where(allowed, similar[:, lane : lane + LANES], -1.0)))
        lines_of(out_ref, jnp.maximum(jnp.concatenate(best, axis=1), cross))

    @pl.when(lax.axis_index("core") != 0)
    def _():
        width = mine_ref.shape[0] - MARKS
        marks = mine_ref[width:].astype(jnp.float32)
        line = marks[0:1] * 16.0 + marks[1:2]
        ranks = jnp.broadcast_to(line, (LANES, line.shape[1])).T
        step = 4 * LANES
        for at in range(0, line.shape[1], step):
            similar = lax.dot_general(
                mine_ref[:width],
                mine_ref[:width, at : at + step],
                TN,
                preferred_element_type=jnp.float32,
            )
            for lane in range(0, step, LANES):
                allowed = ranks < line[:, at + lane : at + lane + LANES]
                best = largest(jnp.where(allowed, similar[:, lane : lane + LANES], -1.0))
                first_ref[:, at + lane : at + lane + LANES] = best


def merge_kernel(first_ref, away_ref, out_ref):
    @pl.when(lax.axis_index("core") != 0)
    def _():
        lines_of(out_ref, jnp.maximum(first_ref[...], away_ref[...]))


def unpack_kernel(best_ref, where_ref, out_ref):
    docs = where_ref.shape[1]
    best = jnp.concatenate([best_ref[...], jnp.zeros((LANES - CLUSTERS, LANES), jnp.float32)])
    cluster = jnp.broadcast_to(where_ref[0:1], (LANES, docs))
    by_cluster = jnp.take_along_axis(best.T, cluster, axis=1)
    wanted = iota((LANES, docs), 0) == where_ref[1:2]
    out_ref[...] = jnp.sum(jnp.where(wanted, by_cluster, 0.0), axis=0, keepdims=True)


def call(kernel, out_shape, flops, moved, **more):
    return pl.pallas_call(
        kernel,
        out_shape=out_shape,
        compiler_params=pltpu.CompilerParams(vmem_limit_bytes=VMEM),
        cost_estimate=pl.CostEstimate(flops=flops, bytes_accessed=moved, transcendentals=0),
        **more,
    )


def in_hbm(x):
    return pltpu.with_memory_space_constraint(x, pltpu.HBM)


def per_device(embeddings, cluster, order):
    docs, width = embeddings.shape
    slots = CLUSTERS * SLOTS
    shape = jax.ShapeDtypeStruct
    f32, bf16, i32 = jnp.float32, jnp.bfloat16, jnp.int32
    tiles = (GROUPS, TILES, 8, LANES)
    moved = CLUSTERS * (SLOTS * width + 2 * LANES) * 2
    packed, where = call(
        pack_kernel,
        (shape(tiles, bf16), shape((8, docs), i32)),
        2 * slots * docs * width,
        docs * width * 4 + moved,
        in_specs=[pl.BlockSpec(memory_space=pltpu.HBM)] * 3,
        scratch_shapes=[
            pltpu.VMEM((docs, width), f32),
            pltpu.VMEM((2, 1, docs), i32),
            pltpu.SemaphoreType.DMA((3,)),
        ],
    )(*(in_hbm(x) for x in (embeddings, cluster.reshape(1, docs), order.reshape(1, docs))))
    chunks = packed.reshape(CLUSTERS, TILES, 2, LANES)

    def exchange(sent):
        return lax.all_to_all(sent, ("x", "zy"), split_axis=0, concat_axis=0, tiled=True)

    def keep(sent):
        return sent

    core = lax.axis_index("core")
    early = lax.cond(core == 1, exchange, keep, chunks)
    late = lax.cond(core == 0, exchange, keep, chunks).reshape(tiles)
    flops = 2 * slots * slots * width
    line = shape((8, slots), f32)
    turned = call(turn_kernel, pltpu.VMEM((width + MARKS, slots), bf16), 0, 2 * moved)(
        pltpu.with_memory_space_constraint(early.reshape(tiles), pltpu.VMEM)
    )
    other = lax.ppermute(turned, "core", [(1, 0)])
    cross, away = call(first_kernel, (shape((slots, LANES), f32), line), flops, 2 * moved)(
        late, other
    )
    away = lax.ppermute(away, "core", [(0, 1), (1, 0)])
    answer = shape((CLUSTERS, LANES), f32)
    mine = pltpu.with_memory_space_constraint(turned, pltpu.VMEM)
    best, first = call(second_kernel, (answer, line), flops, 2 * moved)(late, cross, mine)
    back = lax.cond(core == 0, exchange, keep, best)
    best = call(merge_kernel, answer, 0, CLUSTERS * LANES * 4)(first, away)
    back = lax.cond(core == 1, lambda sent, kept: exchange(sent), lambda sent, kept: kept, best, back)
    result = call(unpack_kernel, shape((1, docs), f32), 0, CLUSTERS * LANES * 4)(back, where)
    return result.reshape(docs)


def solution(mesh):
    devices = mesh.devices.reshape(-1, CORES, mesh.shape["narrow"])
    chips = Mesh(devices, ("zy", "core", "x"))
    axes = ("zy", "core", "x")
    return jax.shard_map(
        per_device,
        mesh=chips,
        in_specs=(P(axes, None), P(axes), P(axes)),
        out_specs=P(axes),
        check_vma=False,
    )
```
